128 devices in a mesh: src: 4 (over x), tile: 32 (over z, y, core).
Axes of the slice: x: 4, y: 4, z: 4, core: 2. Of those that a mesh axis runs over, the one named last changes fastest.
Arguments:
- latent: bfloat16 [3, 128, 16, 160], P(None, ('src', 'tile')), may hold values from -6 to 6
- row_map: int32 [128], replicated, may hold values from 0 to 127, each once
- latent_cache: bfloat16 [2, 128, 16, 160], P(None, 'tile'), may hold values from -6 to 6
- cache_one: bfloat16 [2, 128, 384, 160], P(None, 'tile', 'src'), may hold values from -5 to 5
- cache_two: bfloat16 [2, 128, 384, 160], P(None, 'tile', 'src'), may hold values from -5 to 5
- conv_in_w: bfloat16 [3, 3, 3, 16, 384], P(None, None, None, None, 'src'), may hold values from -0.3125 to 0.3125
- weight_one: bfloat16 [3, 3, 3, 384, 384], P(None, None, None, 'src'), may hold values from -0.0625 to 0.0625
- weight_two: bfloat16 [3, 3, 3, 384, 384], P(None, None, None, 'src'), may hold values from -0.0625 to 0.0625
- gain_one: float32 [384], P('src'), may hold values from 0.1 to 1.9
- gain_two: float32 [384], P('src'), may hold values from 0.1 to 1.9
Outputs:
- decoded: bfloat16 [3, 128, 384, 160], P(None, 'tile', 'src')
The draws below stay inside these ranges and needn't reach their ends.
All inputs are finite; a program needn't handle non-finite values.
Results may differ from the reference program's by a relative error of at most 0.0037.
The reference program's roundings to bfloat16 on the way count: a program that leaves them out, or rounds other values in their place, can miss the bound.
Values may be sent and summed in bfloat16 or wider, within the bound.
A program may use at most 128 MiB of HBM per device.

```python
import jax
import jax.numpy as jnp
from jax import lax

LC = 16
C = 384
GROUPS = 32
LW = 160
FR = 3
GSIZE = 12
LH = 128


def steps_of(stream_key, shape, split, smallest, top_value):
    def one(position, blocks):
        heights = jax.random.uniform(jax.random.fold_in(jax.random.fold_in(stream_key, 6), position), (blocks,), jnp.float32, smallest / len(split), top_value / len(split))
        return jnp.repeat(jnp.exp(heights), shape[position] // blocks).reshape((-1,) + (1,) * (len(shape) - position - 1))

    level = one(*split[0])
    for cut in split[1:]:
        level = level * one(*cut)
    return level


def normal_values(own_key, shape, scale, reach, shards=(), kind=jnp.bfloat16):
    entries = jax.random.normal(own_key, shape, jnp.float32) * scale
    if len(shards) > 0:
        entries = steps_of(own_key, shape, shards, -0.22, 0.18) * entries
    return jnp.clip(entries, min=-reach, max=reach).astype(kind)


def setup_inputs(seed: int = 0) -> dict:
    key_of = jax.random.split(jax.random.key(seed), 11)
    return {
        "latent": normal_values(key_of[0], (FR, LH, LC, LW), 1.0, 6.0, ((1, 128),)),
        "row_map": jax.random.permutation(key_of[1], LH).astype(jnp.int32),
        "latent_cache": normal_values(key_of[2], (2, LH, LC, LW), 1.0, 6.0, ((1, 32),)),
        "cache_one": normal_values(key_of[3], (2, LH, C, LW), 0.7, 5.0, ((1, 32), (2, 4))),
        "cache_two": normal_values(key_of[4], (2, LH, C, LW), 0.7, 5.0, ((1, 32), (2, 4))),
        "conv_in_w": normal_values(key_of[5], (3, 3, 3, LC, C), (27 * LC) ** -0.5, 0.3125, ((4, 4),)),
        "weight_one": normal_values(key_of[6], (3, 3, 3, C, C), (27 * C) ** -0.5, 0.0625, ((3, 4),)),
        "weight_two": normal_values(key_of[7], (3, 3, 3, C, C), (27 * C) ** -0.5, 0.0625, ((3, 4),)),
        "gain_one": jnp.clip(1.0 + 0.18 * jax.random.normal(key_of[8], (C,), jnp.float32), 0.1, 1.9),
        "gain_two": jnp.clip(1.0 + 0.18 * jax.random.normal(key_of[9], (C,), jnp.float32), 0.1, 1.9),
    }


def causal_conv(frames, weight):
    frame_count = frames.shape[0] - 2
    row_count = frames.shape[1]
    columns = frames.shape[3]
    padded = jnp.pad(frames, ((0, 0), (1, 1), (0, 0), (1, 1)))
    summed = jnp.zeros((frame_count, row_count, weight.shape[4], columns), jnp.float32)
    for tap_time in range(3):
        for tap_row in range(3):
            for tap_col in range(3):
                window = padded[tap_time:tap_time + frame_count, tap_row:tap_row + row_count, :, tap_col:tap_col + columns].astype(jnp.float32)
                summed = summed + jnp.einsum('fhcw,co->fhow', window, weight[tap_time, tap_row, tap_col].astype(jnp.float32))
    return summed

def group_norm(hidden, gain):
    frame_count, row_count, channels, columns = hidden.shape
    shaped = hidden.reshape(frame_count, row_count, GROUPS, GSIZE, columns)
    group_mean = lax.optimization_barrier(jnp.mean(shaped, axis=(0, 1, 3, 4), keepdims=True))
    centred = shaped - group_mean
    spread = lax.optimization_barrier(jnp.mean(centred * centred, axis=(0, 1, 3, 4), keepdims=True))
    normed = (centred * lax.rsqrt(spread + 1e-06)).reshape(hidden.shape)
    normed = normed * gain.astype(jnp.float32)[None, None, :, None]
    return jax.nn.silu(normed).astype(jnp.bfloat16)

def reference(latent, row_map, latent_cache, cache_one, cache_two, conv_in_w, weight_one, weight_two, gain_one, gain_two):
    grid = jnp.zeros_like(latent).at[:, row_map].set(latent)
    first = causal_conv(jnp.concatenate([latent_cache, grid], axis=0), conv_in_w).astype(jnp.bfloat16)
    act_one = group_norm(first.astype(jnp.float32), gain_one)
    middle = causal_conv(jnp.concatenate([cache_one, act_one], axis=0), jnp.transpose(weight_one, (0, 1, 2, 4, 3)))
    act_two = group_norm(middle, gain_two)
    last = causal_conv(jnp.concatenate([cache_two, act_two], axis=0), jnp.transpose(weight_two, (0, 1, 2, 4, 3)))
    return (first.astype(jnp.float32) + last).astype(jnp.bfloat16)
```

```python
import functools

import jax
import jax.numpy as jnp
from jax import lax
from jax.experimental import pallas as pl
from jax.experimental.pallas import tpu as pltpu
from jax.sharding import Mesh
from jax.sharding import PartitionSpec as P

GSIZE = 12
GROUPS = 32
AXES = ("src", "z", "y", "core")
TILE = ("z", "y", "core")
SIZES = (4, 4, 4, 2)
MESH = pl.DeviceIdType.MESH
F32 = jnp.float32
BF16 = jnp.bfloat16

TAIL, UP_MAIN, UP_TAIL, DOWN_TAIL, DOWN_MAIN = 3, 5, 6, 7, 8
ROW_SLOT = (4, 0, 1, 2)
SLOT_OF = (UP_MAIN, 4, 0, 1, 2, DOWN_MAIN)
PLANE = tuple((z, y) for z in range(4) for y in range(4) if z or y)


def dot(a, b):
    return lax.dot_general(a, b, (((1,), (0,)), ((), ())), preferred_element_type=F32)


def dot_exact(a, b, dims):
    return lax.dot_general(
        a, b, (dims, ((), ())), precision=lax.Precision.HIGHEST, preferred_element_type=F32
    )


def iota(shape, dim):
    return lax.broadcasted_iota(jnp.int32, shape, dim)


def body(
    entries,
    index_ref,
    latent_ref,
    lcache_ref,
    win_ref,
    gains_ref,
    cache1_hbm,
    cache2_hbm,
    w1_hbm,
    w2_hbm,
    out_ref,
    units,
    rows_all,
    picked,
    lcache,
    shifted,
    win,
    gains,
    stage1,
    stage2,
    w1,
    w2,
    x1,
    x2,
    t1,
    t2,
    acc,
    kept,
    sum1,
    sum2,
    mean_ref,
    scale_ref,
    stat,
    stat_core,
    stat_src,
    send_sem,
    recv_sem,
    local_sem,
):
    s, z, y, core = (lax.axis_index(a) for a in AXES)
    tile = z * 8 + y * 2 + core
    plane = z * 4 + y
    own = pl.ds(pl.multiple_of(s * 96, 96), 96)
    nxt, prv = lax.rem(tile + 1, 32), lax.rem(tile + 31, 32)

    def at_tile(t):
        return (s, t // 8, lax.rem(t // 2, 4), lax.rem(t, 2))

    def src_peer(d):
        return (lax.rem(s + d, 4), z, y, core)

    def plane_peer(k):
        dz, dy = PLANE[k]
        return (s, lax.rem(z + dz, 4), lax.rem(y + dy, 4), core)

    other = (s, z, y, 1 - core)
    counter = [0]

    def remote(src, dst, device):
        k = counter[0]
        counter[0] += 1
        c = pltpu.make_async_remote_copy(
            src_ref=src,
            dst_ref=dst,
            send_sem=send_sem.at[k],
            recv_sem=recv_sem.at[k],
            device_id=device,
            device_id_type=MESH,
        )
        c.start()
        return c

    def local(src, dst, k):
        c = pltpu.make_async_copy(src, dst, local_sem.at[k])
        c.start()
        return c

    sent = []

    def arrived(copies):
        for c in copies:
            c.wait_recv()
        sent.extend(copies)

    def gone():
        for c in sent:
            c.wait_send()
        sent.clear()

    barrier = pltpu.get_barrier_semaphore()
    peers = [src_peer(d) for d in (1, 2, 3)] + [plane_peer(k) for k in range(15)]
    peers += [other, at_tile(nxt), at_tile(prv)]
    for p in peers:
        pl.semaphore_signal(barrier, inc=1, device_id=p, device_id_type=MESH)
    c1 = local(cache1_hbm, stage1, 0)
    c2 = local(cache2_hbm, stage2, 1)
    wl1 = [
        local(w1_hbm.at[:, b], w1.at[:, :, :, pl.ds(b * 384, 384)], 2 + b) for b in range(3)
    ]
    wl2 = [
        local(w2_hbm.at[:, b], w2.at[:, :, :, pl.ds(b * 384, 384)], 5 + b) for b in range(3)
    ]

    from_col, to_col = iota((160, 128), 0), iota((160, 128), 1)

    def tail_place(k):
        hit = (from_col >= 128) & (from_col - 128 == to_col - 32 * k)
        return jnp.where(hit, 1.0, 0.0).astype(BF16)

    place = [tail_place(k) for k in range(4)]

    for f in range(3):
        units[f] = latent_ref[f, :, 0:128]
    tails = sum(dot(latent_ref[f], place[f]) for f in range(3))
    units[3] = tails.astype(BF16)
    base = pl.multiple_of(core * 64 + plane * 4, 4)
    rows_all[base + s] = units[s]
    win[own] = win_ref[...]
    gains[own] = gains_ref[...]
    for f in range(2):
        lcache[f, 2:6] = lcache_ref[f]
    pl.semaphore_wait(barrier, len(peers))

    step0 = [
        remote(units.at[lax.rem(s + d, 4)], rows_all.at[base + s], src_peer(d)) for d in (1, 2, 3)
    ]
    edges = [
        remote(lcache_ref.at[:, 2:4], lcache.at[:, 0:2], at_tile(nxt)),
        remote(lcache_ref.at[:, 0:2], lcache.at[:, 6:8], at_tile(prv)),
    ]
    params = [remote(win_ref, win.at[own], src_peer(d)) for d in (1, 2, 3)]
    params += [remote(gains_ref, gains.at[own], src_peer(d)) for d in (1, 2, 3)]

    def pack_cache(staged, x):
        for f in range(2):
            total = jnp.zeros((96, 128), F32)
            for h in range(4):
                x[f, ROW_SLOT[h], own] = staged[f, h, :, 0:128]
                total = total + dot(staged[f, h], place[h])
            x[f, TAIL, own] = total.astype(BF16)

    def spread(x, frames):
        block = x.at[frames, 0:5, own]
        return [remote(block, block, src_peer(d)) for d in (1, 2, 3)]

    def halo(x, frames):
        return [
            remote(x.at[frames, 2:4], x.at[frames, 5:7], at_tile(nxt)),
            remote(x.at[frames, 3:5], x.at[frames, 7:9], at_tile(prv)),
        ]

    c1.wait()
    pack_cache(stage1, x1)
    arrived(step0)
    mine = rows_all.at[pl.ds(base, 4)]
    step1 = [remote(mine, mine, plane_peer(k)) for k in range(15)]
    cached1 = spread(x1, pl.ds(0, 2))
    c2.wait()
    pack_cache(stage2, x2)

    wide_from, wide_to = iota((160, 256), 0), iota((160, 256), 1)
    shift = jnp.concatenate(
        [jnp.where(wide_from == wide_to + e - 1, 1.0, 0.0).astype(BF16) for e in range(3)], axis=1
    )
    image_row = tile * 4 - 2 + iota((8, 16, 256), 0)
    in_image = (image_row >= 0) & (image_row < 128)

    def put_shifted(f, wide):
        for e in range(3):
            part = wide[:, e * 256 : (e + 1) * 256].reshape(8, 16, 256)
            shifted[f, :, e * 16 : (e + 1) * 16] = jnp.where(in_image, part, 0.0).astype(BF16)

    arrived(edges)
    for f in range(2):
        put_shifted(f, dot(lcache[f].reshape(128, 160), shift))

    arrived(step1)
    half = rows_all.at[pl.ds(pl.multiple_of(core * 64, 64), 64)]
    step2 = [remote(half, half, other)]
    arrived(step2)
    for j in range(8):
        picked[s, j] = rows_all[index_ref[j]]
    step3 = [remote(picked.at[s], picked.at[s], src_peer(d)) for d in (1, 2, 3)]
    arrived(params)
    arrived(step3)
    cached2 = spread(x2, pl.ds(0, 2))
    tail_from, tail_to = iota((128, 256), 0), iota((128, 256), 1)
    for f in range(3):
        tail_shift = []
        for e in range(3):
            j = tail_from - 32 * f
            hit = (j >= 0) & (j < 32) & (128 + j == tail_to + e - 1)
            tail_shift.append(jnp.where(hit, 1.0, 0.0).astype(BF16))
        wide = dot(picked[f].reshape(128, 128), shift[0:128]) + dot(
            picked[3].reshape(128, 128), jnp.concatenate(tail_shift, axis=1)
        )
        put_shifted(2 + f, wide)

    lane = iota((384, 128), 1)
    lane96 = iota((96, 128), 1)
    sum1[...] = jnp.zeros_like(sum1)
    sum2[...] = jnp.zeros_like(sum2)

    @pl.loop(0, 3)
    def _(t):
        tail = jnp.zeros((384, 128), F32)
        for h in range(6):
            window = jnp.concatenate(
                [shifted[t + a, h : h + 3].reshape(144, 256) for a in range(3)], axis=0
            )
            got = dot(win[...], window)
            first = got[:, 0:128].astype(BF16)
            x1[t + 2, SLOT_OF[h]] = first
            ends = got[:, 128:256]
            if h == 0:
                x1[t + 2, UP_TAIL] = pltpu.roll(ends, 96, 1).astype(BF16)
            elif h == 5:
                x1[t + 2, DOWN_TAIL] = ends.astype(BF16)
            else:
                if h > 1:
                    ends = pltpu.roll(ends, 32 * (h - 1), 1)
                hit = (lane >= 32 * (h - 1)) & (lane < 32 * h)
                tail = jnp.where(hit, ends, tail)
                full = first.astype(F32)
                sum1[...] += full
                sum2[...] += full * full
        tail = tail.astype(BF16)
        x1[t + 2, TAIL] = tail
        full = tail.astype(F32)
        sum1[...] += full
        sum2[...] += full * full

    for t in range(3):
        kept[t] = x1[t + 2, 0:5, own]

    channel, group = iota((384, 128), 0), iota((384, 128), 1)

    def member(first_lane):
        low = (group - first_lane) * GSIZE
        hit = (channel >= low) & (channel < low + GSIZE)
        return jnp.where(hit & (group >= first_lane) & (group < first_lane + 32), 1.0, 0.0)

    def stat_row(a, b, rows):
        ones = jnp.ones((8, 128), F32)
        ra = dot_exact(ones, a, ((1,), (1,)))
        rb = dot_exact(ones, b, ((1,), (1,)))
        return ra, rb

    def share_stats(k):
        mine = stat.at[k, core, plane]
        return [remote(mine, mine, plane_peer(i)) for i in range(15)]

    def share_core(k):
        total = stat[k, core, 0]
        for i in range(1, 16):
            total = total + stat[k, core, i]
        stat_core[k, core] = total
        mine = stat_core.at[k, core]
        return [remote(mine, mine, other)]

    def coefficients(total, column):
        mean = total / entries
        square = pltpu.roll(mean, 96, 1)
        spread_ = jnp.maximum(square - mean * mean, 0.0)
        rstd = lax.rsqrt(spread_ + 1e-06)
        one = member(0)
        mean_c = jnp.sum(one * mean[0:1], axis=1, keepdims=True)
        rstd_c = jnp.sum(one * rstd[0:1], axis=1, keepdims=True)
        mean_ref[...] = jnp.broadcast_to(mean_c, (384, 128))
        scale = rstd_c * gains[:, column : column + 1] * 0.5
        scale_ref[...] = jnp.broadcast_to(scale, (384, 128))

    def prepare(x, t, f, norm):
        no_up = jnp.where(tile == 0, 128, 0)
        no_down = jnp.where(tile == 31, 128, 0)
        down_limit = jnp.where(tile == 31, 32, 0)
        up_limit = jnp.where(tile == 0, 96, 128)

        @pl.loop(0, 4)
        def _(c):
            part = pl.ds(pl.multiple_of(c * 96, 96), 96)
            mean, scale = mean_ref[part], scale_ref[part]

            def act(v):
                v = v.astype(F32)
                if not norm:
                    return v
                u = (v - mean) * scale
                return u + u * jnp.tanh(u)

            if norm:
                for slot in ROW_SLOT:
                    x[f, slot, part] = act(x[f, slot, part]).astype(BF16)
            up = act(x[f, UP_MAIN, part])
            x[f, UP_MAIN, part] = jnp.where(lane96 < no_up, 0.0, up).astype(BF16)
            down = act(x[f, DOWN_MAIN, part])
            x[f, DOWN_MAIN, part] = jnp.where(lane96 < no_down, 0.0, down).astype(BF16)
            mid = act(x[f, TAIL, part])
            rim = jnp.where(
                lane96 < 32,
                x[f, DOWN_TAIL, part].astype(F32),
                x[f, UP_TAIL, part].astype(F32),
            )
            rim = act(rim)
            rim = jnp.where((lane96 < down_limit) | (lane96 >= up_limit), 0.0, rim)
            t[f, 1, part] = mid.astype(BF16)
            t[f, 0, part] = pltpu.roll(jnp.where(lane96 >= 96, rim, mid), 32, 1).astype(BF16)
            t[f, 2, part] = pltpu.roll(jnp.where(lane96 < 32, rim, mid), 96, 1).astype(BF16)

    def conv_frame(x, t, w, f):
        low, high = max(0, f - 2), min(2, f)
        count = high - low + 1
        taps = w[low : high + 1].reshape(count * 288, 1152)

        def add(got, i):
            for n, a in enumerate(range(low, high + 1)):
                part = got[n * 288 : (n + 1) * 288]
                if a == 0:
                    acc[f - a, i] = part
                else:
                    acc[f - a, i] += part

        def rows(h):
            return jnp.concatenate([x[f, SLOT_OF[h + b]] for b in range(3)], axis=0)

        for p in range(2):
            got = dot(taps, jnp.concatenate([rows(2 * p), rows(2 * p + 1)], axis=1))
            add(got[:, 0:128], 2 * p)
            add(got[:, 128:256], 2 * p + 1)
        add(dot(taps, t[f].reshape(1152, 128)), 4)

    def combined(t):
        def a(i, e):
            return acc[t, i, e * 96 : (e + 1) * 96]

        before = [pltpu.roll(a(h, 0), 1, 1) for h in range(4)]
        mains = []
        for h in range(4):
            after = jnp.where(
                lane96 == 127, pltpu.roll(a(4, 2), 127 - 32 * h, 1), pltpu.roll(a(h, 2), 127, 1)
            )
            mains.append(a(h, 1) + jnp.where(lane96 == 0, 0.0, before[h]) + after)
        left = pltpu.roll(a(4, 0), 1, 1)
        for h in range(4):
            moved = before[h] if h == 0 else pltpu.roll(before[h], 32 * h, 1)
            left = jnp.where(lane96 == 32 * h, moved, left)
        right = jnp.where((lane96 & 31) == 31, 0.0, pltpu.roll(a(4, 2), 127, 1))
        return mains, a(4, 1) + left + right

    ra, rb = stat_row(sum1[...], sum2[...], 384)
    stat[0, core, plane] = dot_exact(ra, member(0), ((1,), (0,))) + dot_exact(
        rb, member(32), ((1,), (0,))
    )
    shared = share_stats(0)
    arrived(cached1)
    rims = halo(x1, pl.ds(0, 2))
    arrived(shared)
    shared = share_core(0)
    for c in wl1:
        c.wait()
    arrived(rims)
    prepare(x1, t1, 0, False)
    prepare(x1, t1, 1, False)
    conv_frame(x1, t1, w1, 0)
    conv_frame(x1, t1, w1, 1)
    arrived(shared)
    coefficients(stat_core[0, 0] + stat_core[0, 1], 0)

    total1 = jnp.zeros((96, 128), F32)
    total2 = jnp.zeros((96, 128), F32)
    middles = []
    for t in range(3):
        prepare(x1, t1, t + 2, True)
        conv_frame(x1, t1, w1, t + 2)
        mains, tail = combined(t)
        for h in range(4):
            x2[t + 2, ROW_SLOT[h], own] = mains[h].astype(BF16)
        x2[t + 2, TAIL, own] = tail.astype(BF16)
        for v in mains + [tail]:
            total1 = total1 + v
            total2 = total2 + v * v
        middles.append(spread(x2, t + 2))

    ones = jnp.ones((8, 128), F32)
    sum1[...] = jnp.zeros_like(sum1)
    sum2[...] = jnp.zeros_like(sum2)
    sum1[own] = total1
    sum2[own] = total2
    ra, rb = stat_row(sum1[...], sum2[...], 384)
    stat[1, core, plane] = dot_exact(ra, member(0), ((1,), (0,))) + dot_exact(
        rb, member(32), ((1,), (0,))
    )
    shared = share_stats(1)
    arrived(cached2)
    rims2 = halo(x2, pl.ds(0, 2))
    arrived(shared)
    shared = share_core(1)
    for c in wl2:
        c.wait()
    arrived(rims2)
    prepare(x2, t2, 0, False)
    arrived(shared)
    stat_src[s] = stat_core[1, 0] + stat_core[1, 1]
    shared = [remote(stat_src.at[s], stat_src.at[s], src_peer(d)) for d in (1, 2, 3)]
    arrived(middles[0])
    rims = [halo(x2, 2)]
    prepare(x2, t2, 1, False)
    conv_frame(x2, t2, w2, 0)
    arrived(middles[1])
    rims.append(halo(x2, 3))
    conv_frame(x2, t2, w2, 1)
    arrived(shared)
    coefficients(stat_src[0] + stat_src[1] + stat_src[2] + stat_src[3], 1)
    for t in range(3):
        arrived(rims[t])
        gone()
        prepare(x2, t2, t + 2, True)
        conv_frame(x2, t2, w2, t + 2)
        if t == 0:
            arrived(middles[2])
            rims.append(halo(x2, 4))
        mains, tail = combined(t)
        for h in range(4):
            out = kept[t, ROW_SLOT[h]].astype(F32) + mains[h]
            out_ref[t, h, :, 0:128] = out.astype(BF16)
        out = kept[t, TAIL].astype(F32) + tail
        for h in range(4):
            moved = out if h == 0 else pltpu.roll(out, 128 - 32 * h, 1)
            out_ref[t, h, :, 128:160] = moved[:, 0:32].astype(BF16)
    gone()


def per_device(
    latent,
    row_map,
    latent_cache,
    cache_one,
    cache_two,
    conv_in_w,
    weight_one,
    weight_two,
    gain_one,
    gain_two,
):
    frames, _, channels_in, columns = latent.shape
    tile = lax.axis_index(TILE)
    wanted = jnp.clip(tile * 4 - 2 + jnp.arange(8, dtype=jnp.int32), 0, 127)
    places = jnp.arange(128, dtype=jnp.int32)
    t = places % 32
    slot = (t % 2) * 64 + (t // 2) * 4 + places // 32
    index = jnp.sum(
        jnp.where(row_map[None, :] == wanted[:, None], slot[None, :], 0), axis=1, dtype=jnp.int32
    )
    win = conv_in_w.reshape(27 * channels_in, -1).T
    gains = jnp.pad(jnp.stack([gain_one, gain_two], axis=1), ((0, 0), (0, 126)))
    entries = float(frames * 128 * GSIZE * columns)
    vmem = pl.BlockSpec(memory_space=pltpu.VMEM)
    hbm = pl.BlockSpec(memory_space=pl.ANY)
    smem = pl.BlockSpec(memory_space=pltpu.SMEM)
    copies = 3 + 2 + 6 + 15 + 1 + 3 + 3 + 3 + 15 + 2 + 1 + 9 + 15 + 2 + 1 + 3 + 6
    return pl.pallas_call(
        functools.partial(body, entries),
        out_shape=jax.ShapeDtypeStruct((3, 4, 96, 160), BF16),
        in_specs=[smem, vmem, vmem, vmem, vmem, hbm, hbm, hbm, hbm],
        out_specs=vmem,
        scratch_shapes=[
            pltpu.VMEM((4, 16, 128), BF16),
            pltpu.VMEM((128, 16, 128), BF16),
            pltpu.VMEM((4, 8, 16, 128), BF16),
            pltpu.VMEM((2, 8, 16, 160), BF16),
            pltpu.VMEM((5, 8, 48, 256), BF16),
            pltpu.VMEM((384, 432), BF16),
            pltpu.VMEM((384, 128), F32),
            pltpu.VMEM((2, 4, 96, 160), BF16),
            pltpu.VMEM((2, 4, 96, 160), BF16),
            pltpu.VMEM((3, 3, 96, 1152), BF16),
            pltpu.VMEM((3, 3, 96, 1152), BF16),
            pltpu.VMEM((5, 9, 384, 128), BF16),
            pltpu.VMEM((5, 9, 384, 128), BF16),
            pltpu.VMEM((5, 3, 384, 128), BF16),
            pltpu.VMEM((5, 3, 384, 128), BF16),
            pltpu.VMEM((3, 5, 288, 128), F32),
            pltpu.VMEM((3, 5, 96, 128), BF16),
            pltpu.VMEM((384, 128), F32),
            pltpu.VMEM((384, 128), F32),
            pltpu.VMEM((384, 128), F32),
            pltpu.VMEM((384, 128), F32),
            pltpu.VMEM((2, 2, 16, 8, 128), F32),
            pltpu.VMEM((2, 2, 8, 128), F32),
            pltpu.VMEM((4, 8, 128), F32),
            pltpu.SemaphoreType.DMA((copies,)),
            pltpu.SemaphoreType.DMA((copies,)),
            pltpu.SemaphoreType.DMA((8,)),
        ],
        compiler_params=pltpu.CompilerParams(
            collective_id=0, has_side_effects=True, vmem_limit_bytes=56 << 20
        ),
    )(
        index,
        latent.reshape(frames, channels_in, columns),
        latent_cache,
        win,
        gains,
        cache_one,
        cache_two,
        weight_one,
        weight_two,
    )


def solution(mesh):
    torus = Mesh(mesh.devices.reshape(SIZES), AXES)
    all_axes = ("src",) + TILE
    in_specs = (
        P(None, all_axes, None, None),
        P(),
        P(None, TILE, None, None),
        P(None, TILE, "src", None),
        P(None, TILE, "src", None),
        P(None, None, None, None, "src"),
        P(None, None, None, "src", None),
        P(None, None, None, "src", None),
        P("src"),
        P("src"),
    )
    return jax.shard_map(
        per_device,
        mesh=torus,
        in_specs=in_specs,
        out_specs=P(None, TILE, "src", None),
        check_vma=False,
    )
```

```python
import functools

import jax
import jax.numpy as jnp
from jax import lax
from jax.experimental import pallas as pl
from jax.experimental.pallas import tpu as pltpu
from jax.sharding import Mesh
from jax.sharding import PartitionSpec as P

GSIZE = 12
GROUPS = 32
AXES = ("src", "z", "y", "core")
TILE = ("z", "y", "core")
SIZES = (4, 4, 4, 2)
MESH = pl.DeviceIdType.MESH
F32 = jnp.float32
BF16 = jnp.bfloat16

TAIL, UP_MAIN, UP_TAIL, DOWN_TAIL, DOWN_MAIN = 3, 5, 6, 7, 8
ROW_SLOT = (4, 0, 1, 2)
SLOT_OF = (UP_MAIN, 4, 0, 1, 2, DOWN_MAIN)
PLANE = tuple((z, y) for z in range(4) for y in range(4) if z or y)


def dot(a, b):
    return lax.dot_general(a, b, (((1,), (0,)), ((), ())), preferred_element_type=F32)


def dot_t(a, b):
    return lax.dot_general(a, b, (((1,), (1,)), ((), ())), preferred_element_type=F32)


def dot_exact(a, b, dims):
    return lax.dot_general(
        a, b, (dims, ((), ())), precision=lax.Precision.HIGHEST, preferred_element_type=F32
    )


def iota(shape, dim):
    return lax.broadcasted_iota(jnp.int32, shape, dim)


def body(
    entries,
    map_ref,
    latent_ref,
    lcache_ref,
    win_ref,
    gain1_ref,
    gain2_ref,
    cache1_hbm,
    cache2_hbm,
    w1_hbm,
    w2_hbm,
    out_ref,
    units,
    rows_all,
    picked,
    lcache,
    shifted,
    win,
    gains,
    choice,
    stage1,
    stage2,
    w1,
    w2,
    x1,
    x2,
    t1,
    t2,
    acc,
    kept,
    sum1,
    sum2,
    mean_ref,
    scale_ref,
    stat,
    stat_ring,
    send_sem,
    recv_sem,
    local_sem,
):
    s, z, y, core = (lax.axis_index(a) for a in AXES)
    tile = z * 8 + y * 2 + core
    plane = z * 4 + y
    own = pl.ds(pl.multiple_of(s * 96, 96), 96)
    nxt, prv = lax.rem(tile + 1, 32), lax.rem(tile + 31, 32)

    def at_tile(t):
        return (s, t // 8, lax.rem(t // 2, 4), lax.rem(t, 2))

    def src_peer(d):
        return (lax.rem(s + d, 4), z, y, core)

    def plane_peer(k):
        dz, dy = PLANE[k]
        return (s, lax.rem(z + dz, 4), lax.rem(y + dy, 4), core)

    other = (s, z, y, 1 - core)

    def ring_peer(i):
        if i < 3:
            return src_peer(i + 1)
        return (lax.rem(s + i - 3, 4), z, y, 1 - core)

    counter = [0]

    def remote(src, dst, device):
        k = counter[0]
        counter[0] += 1
        c = pltpu.make_async_remote_copy(
            src_ref=src,
            dst_ref=dst,
            send_sem=send_sem.at[k],
            recv_sem=recv_sem.at[k],
            device_id=device,
            device_id_type=MESH,
        )
        c.start()
        return c

    def local(src, dst, k):
        c = pltpu.make_async_copy(src, dst, local_sem.at[k])
        c.start()
        return c

    sent = []

    def arrived(copies):
        for c in copies:
            c.wait_recv()
        sent.extend(copies)

    def gone():
        for c in sent:
            c.wait_send()
        sent.clear()

    barrier = pltpu.get_barrier_semaphore()
    peers = [src_peer(d) for d in (1, 2, 3)] + [plane_peer(k) for k in range(15)]
    peers += [ring_peer(i) for i in range(3, 7)] + [at_tile(nxt), at_tile(prv)]
    for p in peers:
        pl.semaphore_signal(barrier, inc=1, device_id=p, device_id_type=MESH)
    c1 = local(cache1_hbm, stage1, 0)
    c2 = local(cache2_hbm, stage2, 1)
    wl1 = [
        local(w1_hbm.at[:, b], w1.at[:, :, :, pl.ds(b * 384, 384)], 2 + b) for b in range(3)
    ]
    wl2 = [
        local(w2_hbm.at[:, b], w2.at[:, :, :, pl.ds(b * 384, 384)], 5 + b) for b in range(3)
    ]

    from_col, to_col = iota((160, 128), 0), iota((160, 128), 1)

    def tail_place(k):
        hit = (from_col >= 128) & (from_col - 128 == to_col - 32 * k)
        return jnp.where(hit, 1.0, 0.0).astype(BF16)

    place = [tail_place(k) for k in range(3)]

    for f in range(3):
        units[f] = latent_ref[f, :, 0:128]
    tails = sum(dot(latent_ref[f], place[f]) for f in range(3))
    units[3] = tails.astype(BF16)
    base = pl.multiple_of(core * 64 + plane * 4, 4)
    rows_all[base + s] = units[s]
    eye = jnp.where(iota((96, 96), 0) == iota((96, 96), 1), 1.0, 0.0).astype(BF16)
    taps_in = dot_t(eye, win_ref[...]).astype(BF16)
    win[0, s] = taps_in[0:48]
    win[1, s] = taps_in[48:96]
    gains[s] = jnp.zeros((8, 128), F32)
    gains[s, 0:1, 0:96] = gain1_ref[...]
    gains[s, 1:2, 0:96] = gain2_ref[...]
    for f in range(2):
        lcache[f, 2:6] = lcache_ref[f]
    def pack_cache(staged, x):
        for f in range(2):
            for h in range(4):
                x[f, ROW_SLOT[h], own] = dot_t(eye, staged[f, h, 0:128]).astype(BF16)
            tails = jnp.concatenate([staged[f, h, 128:160] for h in range(4)], axis=0)
            x[f, TAIL, own] = dot_t(eye, tails).astype(BF16)

    c1.wait()
    pack_cache(stage1, x1)
    pl.semaphore_wait(barrier, len(peers))

    step0 = [
        remote(units.at[lax.rem(s + d, 4)], rows_all.at[base + s], src_peer(d)) for d in (1, 2, 3)
    ]
    edges = [
        remote(lcache_ref.at[:, 2:4], lcache.at[:, 0:2], at_tile(nxt)),
        remote(lcache_ref.at[:, 0:2], lcache.at[:, 6:8], at_tile(prv)),
    ]
    params = [remote(gains.at[s], gains.at[s], src_peer(d)) for d in (1, 2, 3)]

    def spread(x, frames):
        block = x.at[frames, 0:5, own]
        return [remote(block, block, src_peer(d)) for d in (1, 3)]

    def relay(x, frames):
        copies = []
        for d, first in ((1, 0), (3, 48)):
            part = pl.ds(pl.multiple_of(lax.rem(s + 4 - d, 4) * 96 + first, 16), 48)
            block = x.at[frames, 0:5, part]
            copies.append(remote(block, block, src_peer(d)))
        return copies

    def halo(x, frames):
        return [
            remote(x.at[frames, 2:4], x.at[frames, 5:7], at_tile(nxt)),
            remote(x.at[frames, 3:5], x.at[frames, 7:9], at_tile(prv)),
        ]

    cached1 = spread(x1, pl.ds(0, 2))
    mine = win.at[core, s]
    params += [remote(mine, mine, src_peer(d)) for d in (1, 2, 3)]
    arrived(step0)
    mine = rows_all.at[pl.ds(base, 4)]
    step1 = [remote(mine, mine, plane_peer(k)) for k in range(15)]
    c2.wait()
    pack_cache(stage2, x2)
    place_of, slot_of = iota((128, 2048), 0), iota((128, 2048), 1) // 16
    held = (lax.rem(slot_of, 4) * 32) + lax.rem(slot_of // 4, 16) * 2 + slot_of // 64
    holds = jnp.where(place_of == held, 1.0, 0.0).astype(BF16)
    image_rows = jnp.broadcast_to(map_ref[...].astype(F32), (8, 128)).astype(BF16)
    row_at = dot(image_rows, holds)[0:1].astype(jnp.int32)
    wanted = jnp.clip(tile * 4 - 2 + iota((128, 2048), 0) // 16, 0, 127)
    same = lax.rem(iota((128, 2048), 0), 16) == lax.rem(iota((128, 2048), 1), 16)
    choice[...] = jnp.where((row_at == wanted) & same, 1.0, 0.0).astype(BF16)

    wide_from, wide_to = iota((160, 256), 0), iota((160, 256), 1)
    shift = jnp.concatenate(
        [jnp.where(wide_from == wide_to + e - 1, 1.0, 0.0).astype(BF16) for e in range(3)], axis=1
    )
    image_row = tile * 4 - 2 + iota((8, 16, 256), 0)
    in_image = (image_row >= 0) & (image_row < 128)

    def put_shifted(f, wide):
        for e in range(3):
            part = wide[:, e * 256 : (e + 1) * 256].reshape(8, 16, 256)
            shifted[f, :, e * 16 : (e + 1) * 16] = jnp.where(in_image, part, 0.0).astype(BF16)

    arrived(edges)
    for f in range(2):
        put_shifted(f, dot(lcache[f].reshape(128, 160), shift))

    arrived(cached1)
    arrived(step1)
    half = rows_all.at[pl.ds(pl.multiple_of(core * 64, 64), 64)]
    step2 = [remote(half, half, other)]
    cached1 = relay(x1, pl.ds(0, 2))
    arrived(step2)
    chosen = dot(choice[...], rows_all[...].reshape(2048, 128))
    picked[s] = chosen.astype(BF16).reshape(8, 16, 128)
    step3 = [remote(picked.at[s], picked.at[s], src_peer(d)) for d in (1, 2, 3)]
    cached2 = spread(x2, pl.ds(0, 2))
    arrived(params)
    params = [remote(win.at[core], win.at[core], other)]
    arrived(step3)
    arrived(cached1)
    rims = halo(x1, pl.ds(0, 2))
    tail_from, tail_to = iota((128, 256), 0), iota((128, 256), 1)
    for f in range(3):
        tail_shift = []
        for e in range(3):
            j = tail_from - 32 * f
            hit = (j >= 0) & (j < 32) & (128 + j == tail_to + e - 1)
            tail_shift.append(jnp.where(hit, 1.0, 0.0).astype(BF16))
        wide = dot(picked[f].reshape(128, 128), shift[0:128]) + dot(
            picked[3].reshape(128, 128), jnp.concatenate(tail_shift, axis=1)
        )
        put_shifted(2 + f, wide)

    arrived(params)
    lane = iota((384, 128), 1)
    lane96 = iota((96, 128), 1)
    sum1[...] = jnp.zeros_like(sum1)
    sum2[...] = jnp.zeros_like(sum2)

    def all_taps():
        return jnp.concatenate([win[i % 2, i // 2] for i in range(8)], axis=0)

    @pl.loop(0, 3)
    def _(t):
        tail = jnp.zeros((384, 128), F32)
        for h in range(6):
            window = jnp.concatenate(
                [shifted[t + a, h : h + 3].reshape(144, 256) for a in range(3)], axis=0
            )
            got = dot(all_taps(), window)
            first = got[:, 0:128].astype(BF16)
            x1[t + 2, SLOT_OF[h]] = first
            ends = got[:, 128:256]
            if h == 0:
                x1[t + 2, UP_TAIL] = pltpu.roll(ends, 96, 1).astype(BF16)
            elif h == 5:
                x1[t + 2, DOWN_TAIL] = ends.astype(BF16)
            else:
                if h > 1:
                    ends = pltpu.roll(ends, 32 * (h - 1), 1)
                hit = (lane >= 32 * (h - 1)) & (lane < 32 * h)
                tail = jnp.where(hit, ends, tail)
                full = first.astype(F32)
                sum1[...] += full
                sum2[...] += full * full
        tail = tail.astype(BF16)
        x1[t + 2, TAIL] = tail
        full = tail.astype(F32)
        sum1[...] += full
        sum2[...] += full * full

    for t in range(3):
        kept[t] = x1[t + 2, 0:5, own]

    channel, group = iota((384, 128), 0), iota((384, 128), 1)

    def member(first_lane):
        low = (group - first_lane) * GSIZE
        hit = (channel >= low) & (channel < low + GSIZE)
        return jnp.where(hit & (group >= first_lane) & (group < first_lane + 32), 1.0, 0.0)

    def stat_row(a, b, rows):
        ones = jnp.ones((8, 128), F32)
        ra = dot_exact(ones, a, ((1,), (1,)))
        rb = dot_exact(ones, b, ((1,), (1,)))
        return ra, rb

    def share_ring(k, peers_):
        mine = stat_ring.at[k, s, core]
        return [remote(mine, mine, ring_peer(i)) for i in peers_]

    def share_plane(k):
        mine = stat.at[k, plane]
        return [remote(mine, mine, plane_peer(i)) for i in range(15)]

    def plane_total(k):
        total = stat[k, 0]
        for i in range(1, 16):
            total = total + stat[k, i]
        return total

    def coefficients(total, column):
        mean = total / entries
        square = pltpu.roll(mean, 96, 1)
        spread_ = jnp.maximum(square - mean * mean, 0.0)
        rstd = lax.rsqrt(spread_ + 1e-06)
        one = member(0)
        mean_c = jnp.sum(one * mean[0:1], axis=1, keepdims=True)
        rstd_c = jnp.sum(one * rstd[0:1], axis=1, keepdims=True)
        mean_ref[...] = jnp.broadcast_to(mean_c, (384, 128))
        eye32 = jnp.where(lane96 == iota((96, 128), 0), 1.0, 0.0)
        gain_c = jnp.concatenate(
            [
                jnp.sum(eye32 * gains[i, column : column + 1], axis=1, keepdims=True)
                for i in range(4)
            ],
            axis=0,
        )
        scale = rstd_c * gain_c * 0.5
        scale_ref[...] = jnp.broadcast_to(scale, (384, 128))

    def prepare(x, t, f, norm):
        no_up = jnp.where(tile == 0, 128, 0)
        no_down = jnp.where(tile == 31, 128, 0)
        down_limit = jnp.where(tile == 31, 32, 0)
        up_limit = jnp.where(tile == 0, 96, 128)

        @pl.loop(0, 4)
        def _(c):
            part = pl.ds(pl.multiple_of(c * 96, 96), 96)
            mean, scale = mean_ref[part], scale_ref[part]

            def act(v):
                v = v.astype(F32)
                if not norm:
                    return v
                u = (v - mean) * scale
                return u + u * jnp.tanh(u)

            if norm:
                for slot in ROW_SLOT:
                    x[f, slot, part] = act(x[f, slot, part]).astype(BF16)
            up = act(x[f, UP_MAIN, part])
            x[f, UP_MAIN, part] = jnp.where(lane96 < no_up, 0.0, up).astype(BF16)
            down = act(x[f, DOWN_MAIN, part])
            x[f, DOWN_MAIN, part] = jnp.where(lane96 < no_down, 0.0, down).astype(BF16)
            mid = act(x[f, TAIL, part])
            rim = jnp.where(
                lane96 < 32,
                x[f, DOWN_TAIL, part].astype(F32),
                x[f, UP_TAIL, part].astype(F32),
            )
            rim = act(rim)
            rim = jnp.where((lane96 < down_limit) | (lane96 >= up_limit), 0.0, rim)
            t[f, 1, part] = mid.astype(BF16)
            t[f, 0, part] = pltpu.roll(jnp.where(lane96 >= 96, rim, mid), 32, 1).astype(BF16)
            t[f, 2, part] = pltpu.roll(jnp.where(lane96 < 32, rim, mid), 96, 1).astype(BF16)

    def conv_frame(x, t, w, f, low, high):
        count = high - low + 1
        taps = w[low : high + 1].reshape(count * 288, 1152)

        def add(got, i):
            for n, a in enumerate(range(low, high + 1)):
                part = got[n * 288 : (n + 1) * 288]
                if a == 0:
                    acc[f - a, i] = part
                else:
                    acc[f - a, i] += part

        def rows(h):
            return jnp.concatenate([x[f, SLOT_OF[h + b]] for b in range(3)], axis=0)

        for p in range(2):
            got = dot(taps, jnp.concatenate([rows(2 * p), rows(2 * p + 1)], axis=1))
            add(got[:, 0:128], 2 * p)
            add(got[:, 128:256], 2 * p + 1)
        add(dot(taps, t[f].reshape(1152, 128)), 4)

    def combined(t):
        def a(i, e):
            return acc[t, i, e * 96 : (e + 1) * 96]

        before = [pltpu.roll(a(h, 0), 1, 1) for h in range(4)]
        mains = []
        for h in range(4):
            after = jnp.where(
                lane96 == 127, pltpu.roll(a(4, 2), 127 - 32 * h, 1), pltpu.roll(a(h, 2), 127, 1)
            )
            mains.append(a(h, 1) + jnp.where(lane96 == 0, 0.0, before[h]) + after)
        left = pltpu.roll(a(4, 0), 1, 1)
        for h in range(4):
            moved = before[h] if h == 0 else pltpu.roll(before[h], 32 * h, 1)
            left = jnp.where(lane96 == 32 * h, moved, left)
        right = jnp.where((lane96 & 31) == 31, 0.0, pltpu.roll(a(4, 2), 127, 1))
        return mains, a(4, 1) + left + right

    ra, rb = stat_row(sum1[...], sum2[...], 384)
    stat_ring[0, s, core] = dot_exact(ra, member(0), ((1,), (0,))) + dot_exact(
        rb, member(32), ((1,), (0,))
    )
    shared = share_ring(0, (3,))
    for c in wl1:
        c.wait()
    arrived(rims)
    arrived(shared)
    stat[0, plane] = stat_ring[0, s, 0] + stat_ring[0, s, 1]
    shared = share_plane(0)
    for f in range(2):
        prepare(x1, t1, f, False)
        conv_frame(x1, t1, w1, f, 0, f)
    arrived(cached2)
    cached2 = relay(x2, pl.ds(0, 2))
    arrived(shared)
    coefficients(plane_total(0), 0)

    total1 = jnp.zeros((96, 128), F32)
    total2 = jnp.zeros((96, 128), F32)
    middles = []
    for t in range(3):
        prepare(x1, t1, t + 2, True)
        if t == 1:
            conv_frame(x1, t1, w1, 2, 0, 1)
        if t == 2:
            conv_frame(x1, t1, w1, 3, 1, 1)
        conv_frame(x1, t1, w1, t + 2, 2, 2)
        mains, tail = combined(t)
        for h in range(4):
            x2[t + 2, ROW_SLOT[h], own] = mains[h].astype(BF16)
        x2[t + 2, TAIL, own] = tail.astype(BF16)
        for v in mains + [tail]:
            total1 = total1 + v
            total2 = total2 + v * v
        middles.append(spread(x2, t + 2))
        if t == 0:
            arrived(cached2)
            rims2 = halo(x2, pl.ds(0, 2))

    sum1[...] = jnp.zeros_like(sum1)
    sum2[...] = jnp.zeros_like(sum2)
    sum1[own] = total1
    sum2[own] = total2
    ra, rb = stat_row(sum1[...], sum2[...], 384)
    stat_ring[1, s, core] = dot_exact(ra, member(0), ((1,), (0,))) + dot_exact(
        rb, member(32), ((1,), (0,))
    )
    shared = share_ring(1, range(7))
    for c in wl2:
        c.wait()
    arrived(rims2)
    for f in range(2):
        prepare(x2, t2, f, False)
    conv_frame(x2, t2, w2, 0, 0, 0)
    arrived(middles[0])
    middles[0] = relay(x2, 2)
    arrived(shared)
    total = stat_ring[1, 0, 0] + stat_ring[1, 0, 1]
    for i in range(1, 4):
        total = total + (stat_ring[1, i, 0] + stat_ring[1, i, 1])
    stat[1, plane] = total
    shared = share_plane(1)
    arrived(middles[1])
    middles[1] = relay(x2, 3)
    conv_frame(x2, t2, w2, 1, 0, 1)
    arrived(middles[0])
    rims = [halo(x2, 2)]
    arrived(middles[2])
    middles[2] = relay(x2, 4)
    arrived(shared)
    coefficients(plane_total(1), 1)
    eye128 = jnp.where(iota((128, 128), 0) == iota((128, 128), 1), 1.0, 0.0).astype(BF16)
    for t in range(3):
        arrived(rims[t])
        gone()
        prepare(x2, t2, t + 2, True)
        if t == 0:
            arrived(middles[1])
            rims.append(halo(x2, 3))
        conv_frame(x2, t2, w2, t + 2, t, 2)
        if t == 0:
            arrived(middles[2])
            rims.append(halo(x2, 4))
        mains, tail = combined(t)
        for h in range(4):
            out = (kept[t, ROW_SLOT[h]].astype(F32) + mains[h]).astype(BF16)
            out_ref[t, h, 0:128] = dot_t(eye128, out).astype(BF16)
        out = (kept[t, TAIL].astype(F32) + tail).astype(BF16)
        turned = dot_t(eye128, out).astype(BF16)
        for h in range(4):
            out_ref[t, h, 128:160] = turned[32 * h : 32 * h + 32]
    gone()


def per_device(
    latent,
    row_map,
    latent_cache,
    cache_one,
    cache_two,
    conv_in_w,
    weight_one,
    weight_two,
    gain_one,
    gain_two,
):
    frames, _, channels_in, columns = latent.shape
    entries = float(frames * 128 * GSIZE * columns)
    vmem = pl.BlockSpec(memory_space=pltpu.VMEM)
    hbm = pl.BlockSpec(memory_space=pl.ANY)
    copies = 3 + 2 + 7 + 15 + 1 + 3 + 4 + 4 + 2 + 1 + 15 + 12 + 2 + 7 + 15 + 6
    decoded = pl.pallas_call(
        functools.partial(body, entries),
        out_shape=jax.ShapeDtypeStruct((3, 4, 160, 96), BF16),
        in_specs=[vmem, vmem, vmem, vmem, vmem, vmem, hbm, hbm, hbm, hbm],
        out_specs=vmem,
        scratch_shapes=[
            pltpu.VMEM((4, 16, 128), BF16),
            pltpu.VMEM((128, 16, 128), BF16),
            pltpu.VMEM((4, 8, 16, 128), BF16),
            pltpu.VMEM((2, 8, 16, 160), BF16),
            pltpu.VMEM((5, 8, 48, 256), BF16),
            pltpu.VMEM((2, 4, 48, 432), BF16),
            pltpu.VMEM((4, 8, 128), F32),
            pltpu.VMEM((128, 2048), BF16),
            pltpu.VMEM((2, 4, 160, 96), BF16),
            pltpu.VMEM((2, 4, 160, 96), BF16),
            pltpu.VMEM((3, 3, 96, 1152), BF16),
            pltpu.VMEM((3, 3, 96, 1152), BF16),
            pltpu.VMEM((5, 9, 384, 128), BF16),
            pltpu.VMEM((5, 9, 384, 128), BF16),
            pltpu.VMEM((5, 3, 384, 128), BF16),
            pltpu.VMEM((5, 3, 384, 128), BF16),
            pltpu.VMEM((3, 5, 288, 128), F32),
            pltpu.VMEM((3, 5, 96, 128), BF16),
            pltpu.VMEM((384, 128), F32),
            pltpu.VMEM((384, 128), F32),
            pltpu.VMEM((384, 128), F32),
            pltpu.VMEM((384, 128), F32),
            pltpu.VMEM((2, 16, 8, 128), F32),
            pltpu.VMEM((2, 4, 2, 8, 128), F32),
            pltpu.SemaphoreType.DMA((copies,)),
            pltpu.SemaphoreType.DMA((copies,)),
            pltpu.SemaphoreType.DMA((8,)),
        ],
        compiler_params=pltpu.CompilerParams(
            collective_id=0, has_side_effects=True, vmem_limit_bytes=56 << 20
        ),
    )(
        row_map.reshape(1, 128),
        latent.reshape(frames, channels_in, columns),
        latent_cache,
        conv_in_w.reshape(27 * channels_in, 96),
        gain_one.reshape(1, 96),
        gain_two.reshape(1, 96),
        jnp.swapaxes(cache_one, 2, 3),
        jnp.swapaxes(cache_two, 2, 3),
        weight_one,
        weight_two,
    )
    return jnp.swapaxes(decoded, 2, 3)


def solution(mesh):
    torus = Mesh(mesh.devices.reshape(SIZES), AXES)
    all_axes = ("src",) + TILE
    in_specs = (
        P(None, all_axes, None, None),
        P(),
        P(None, TILE, None, None),
        P(None, TILE, "src", None),
        P(None, TILE, "src", None),
        P(None, None, None, None, "src"),
        P(None, None, None, "src", None),
        P(None, None, None, "src", None),
        P("src"),
        P("src"),
    )
    return jax.shard_map(
        per_device,
        mesh=torus,
        in_specs=in_specs,
        out_specs=P(None, TILE, "src", None),
        check_vma=False,
    )
```

```python
import functools

import jax
import jax.numpy as jnp
from jax import lax
from jax.experimental import pallas as pl
from jax.experimental.pallas import tpu as pltpu
from jax.sharding import Mesh
from jax.sharding import PartitionSpec as P

GSIZE = 12
GROUPS = 32
AXES = ("src", "z", "y", "core")
TILE = ("z", "y", "core")
SIZES = (4, 4, 4, 2)
MESH = pl.DeviceIdType.MESH
F32 = jnp.float32
BF16 = jnp.bfloat16

TAIL, UP_MAIN, UP_TAIL, DOWN_TAIL, DOWN_MAIN = 3, 5, 6, 7, 8
ROW_SLOT = (4, 0, 1, 2)
SLOT_OF = (UP_MAIN, 4, 0, 1, 2, DOWN_MAIN)
PLANE = tuple((z, y) for z in range(4) for y in range(4) if z or y)


def dot(a, b):
    return lax.dot_general(a, b, (((1,), (0,)), ((), ())), preferred_element_type=F32)


def dot_t(a, b):
    return lax.dot_general(a, b, (((1,), (1,)), ((), ())), preferred_element_type=F32)


def dot_exact(a, b, dims):
    return lax.dot_general(
        a, b, (dims, ((), ())), precision=lax.Precision.HIGHEST, preferred_element_type=F32
    )


def iota(shape, dim):
    return lax.broadcasted_iota(jnp.int32, shape, dim)


def body(
    entries,
    map_ref,
    latent_ref,
    lcache_ref,
    win_ref,
    gain1_ref,
    gain2_ref,
    cache1_hbm,
    cache2_hbm,
    w1_hbm,
    w2_hbm,
    out_ref,
    units,
    rows_all,
    picked,
    lcache,
    shifted,
    win,
    gains,
    choice,
    stage1,
    stage2,
    w1,
    w2,
    x1,
    x2,
    t1,
    t2,
    acc,
    kept,
    sum1,
    sum2,
    mean_ref,
    scale_ref,
    stat,
    stat_ring,
    send_sem,
    recv_sem,
    local_sem,
):
    s, z, y, core = (lax.axis_index(a) for a in AXES)
    tile = z * 8 + y * 2 + core
    plane = z * 4 + y
    own = pl.ds(pl.multiple_of(s * 96, 96), 96)
    nxt, prv = lax.rem(tile + 1, 32), lax.rem(tile + 31, 32)

    def at_tile(t):
        return (s, t // 8, lax.rem(t // 2, 4), lax.rem(t, 2))

    def src_peer(d):
        return (lax.rem(s + d, 4), z, y, core)

    def plane_peer(k):
        dz, dy = PLANE[k]
        return (s, lax.rem(z + dz, 4), lax.rem(y + dy, 4), core)

    other = (s, z, y, 1 - core)

    def ring_peer(i):
        if i < 3:
            return src_peer(i + 1)
        return (lax.rem(s + i - 3, 4), z, y, 1 - core)

    counter = [0]

    def taken(count):
        counter[0] += count
        return counter[0] - count

    def copy_of(k, src, dst, device):
        return pltpu.make_async_remote_copy(
            src_ref=src,
            dst_ref=dst,
            send_sem=send_sem.at[k],
            recv_sem=recv_sem.at[k],
            device_id=device,
            device_id_type=MESH,
        )

    def remote(src, dst, device):
        c = copy_of(taken(1), src, dst, device)
        c.start()
        return c

    def remotes(moves):
        return [remote(*move) for move in moves]

    def local(src, dst, k):
        c = pltpu.make_async_copy(src, dst, local_sem.at[k])
        c.start()
        return c

    sent = []

    def arrived(copies):
        for c in copies:
            c.wait_recv()
        sent.extend(copies)

    def gone():
        for c in sent:
            c.wait_send()
        sent.clear()

    barrier = pltpu.get_barrier_semaphore()
    peers = [src_peer(d) for d in (1, 2, 3)] + [plane_peer(k) for k in range(15)]
    peers += [ring_peer(i) for i in range(3, 7)] + [at_tile(nxt), at_tile(prv)]
    for p in peers:
        pl.semaphore_signal(barrier, inc=1, device_id=p, device_id_type=MESH)
    c1 = local(cache1_hbm, stage1, 0)
    c2 = local(cache2_hbm, stage2, 1)
    wl1 = [
        local(w1_hbm.at[:, b], w1.at[:, :, :, pl.ds(b * 384, 384)], 2 + b) for b in range(3)
    ]
    wl2 = [
        local(w2_hbm.at[:, b], w2.at[:, :, :, pl.ds(b * 384, 384)], 5 + b) for b in range(3)
    ]

    from_col, to_col = iota((160, 128), 0), iota((160, 128), 1)

    def tail_place(k):
        hit = (from_col >= 128) & (from_col - 128 == to_col - 32 * k)
        return jnp.where(hit, 1.0, 0.0).astype(BF16)

    place = [tail_place(k) for k in range(3)]

    for f in range(3):
        units[f] = latent_ref[f, :, 0:128]
    tails = sum(dot(latent_ref[f], place[f]) for f in range(3))
    units[3] = tails.astype(BF16)
    base = pl.multiple_of(core * 64 + plane * 4, 4)
    rows_all[base + s] = units[s]
    eye = jnp.where(iota((96, 96), 0) == iota((96, 96), 1), 1.0, 0.0).astype(BF16)
    taps_in = dot_t(eye, win_ref[...]).astype(BF16)
    win[0, s] = taps_in[0:48]
    win[1, s] = taps_in[48:96]
    gains[s] = jnp.zeros((8, 128), F32)
    gains[s, 0:1, 0:96] = gain1_ref[...]
    gains[s, 1:2, 0:96] = gain2_ref[...]
    acc[...] = jnp.zeros_like(acc)
    for f in range(2):
        lcache[f, 2:6] = lcache_ref[f]
    def pack_cache(staged, x):
        for f in range(2):
            for h in range(4):
                x[f, ROW_SLOT[h], own] = dot_t(eye, staged[f, h, 0:128]).astype(BF16)
            tails = jnp.concatenate([staged[f, h, 128:160] for h in range(4)], axis=0)
            x[f, TAIL, own] = dot_t(eye, tails).astype(BF16)

    c1.wait()
    pack_cache(stage1, x1)
    pl.semaphore_wait(barrier, len(peers))

    step0 = [
        remote(units.at[lax.rem(s + d, 4)], rows_all.at[base + s], src_peer(d)) for d in (1, 2, 3)
    ]
    edges = [
        remote(lcache_ref.at[:, 2:4], lcache.at[:, 0:2], at_tile(nxt)),
        remote(lcache_ref.at[:, 0:2], lcache.at[:, 6:8], at_tile(prv)),
    ]
    params = [remote(gains.at[s], gains.at[s], src_peer(d)) for d in (1, 2, 3)]

    def spread(x, frames):
        block = x.at[frames, 0:5, own]
        return [(block, block, src_peer(d)) for d in (1, 3)]

    def relay(x, frames):
        moves = []
        for d, first in ((1, 0), (3, 48)):
            part = pl.ds(pl.multiple_of(lax.rem(s + 4 - d, 4) * 96 + first, 16), 48)
            block = x.at[frames, 0:5, part]
            moves.append((block, block, src_peer(d)))
        return moves

    def halo(x, frames):
        return [
            (x.at[frames, 2:4], x.at[frames, 5:7], at_tile(nxt)),
            (x.at[frames, 3:5], x.at[frames, 7:9], at_tile(prv)),
        ]

    def block_halo(x, frames, ways):
        moves = []
        for d in ways:
            part = pl.ds(pl.multiple_of(lax.rem(s + d, 4) * 96, 96), 96)
            moves += [
                (x.at[frames, 2:4, part], x.at[frames, 5:7, part], at_tile(nxt)),
                (x.at[frames, 3:5, part], x.at[frames, 7:9, part], at_tile(prv)),
            ]
        return moves

    cached1 = remotes(spread(x1, pl.ds(0, 2)))
    mine = win.at[core, s]
    params += [remote(mine, mine, src_peer(d)) for d in (1, 2, 3)]
    arrived(step0)
    mine = rows_all.at[pl.ds(base, 4)]
    step1 = [remote(mine, mine, plane_peer(k)) for k in range(15)]
    c2.wait()
    pack_cache(stage2, x2)
    place_of, slot_of = iota((128, 2048), 0), iota((128, 2048), 1) // 16
    held = (lax.rem(slot_of, 4) * 32) + lax.rem(slot_of // 4, 16) * 2 + slot_of // 64
    holds = jnp.where(place_of == held, 1.0, 0.0).astype(BF16)
    image_rows = jnp.broadcast_to(map_ref[...].astype(F32), (8, 128)).astype(BF16)
    row_at = dot(image_rows, holds)[0:1].astype(jnp.int32)
    wanted = jnp.clip(tile * 4 - 2 + iota((128, 2048), 0) // 16, 0, 127)
    same = lax.rem(iota((128, 2048), 0), 16) == lax.rem(iota((128, 2048), 1), 16)
    choice[...] = jnp.where((row_at == wanted) & same, 1.0, 0.0).astype(BF16)

    wide_from, wide_to = iota((160, 256), 0), iota((160, 256), 1)
    shift = jnp.concatenate(
        [jnp.where(wide_from == wide_to + e - 1, 1.0, 0.0).astype(BF16) for e in range(3)], axis=1
    )
    image_row = tile * 4 - 2 + iota((8, 16, 256), 0)
    in_image = (image_row >= 0) & (image_row < 128)

    def put_shifted(f, wide):
        for e in range(3):
            part = wide[:, e * 256 : (e + 1) * 256].reshape(8, 16, 256)
            shifted[f, :, e * 16 : (e + 1) * 16] = jnp.where(in_image, part, 0.0).astype(BF16)

    arrived(edges)
    for f in range(2):
        put_shifted(f, dot(lcache[f].reshape(128, 160), shift))

    arrived(cached1)
    arrived(step1)
    half = rows_all.at[pl.ds(pl.multiple_of(core * 64, 64), 64)]
    step2 = [remote(half, half, other)]
    cached1 = remotes(relay(x1, pl.ds(0, 2)))
    arrived(step2)
    chosen = dot(choice[...], rows_all[...].reshape(2048, 128))
    picked[s] = chosen.astype(BF16).reshape(8, 16, 128)
    step3 = [remote(picked.at[s], picked.at[s], src_peer(d)) for d in (1, 2, 3)]
    arrived(params)
    params = [remote(win.at[core], win.at[core], other)]
    arrived(step3)
    cached2 = remotes(spread(x2, pl.ds(0, 2)))
    arrived(cached1)
    rims = remotes(halo(x1, pl.ds(0, 2)))
    tail_from, tail_to = iota((128, 256), 0), iota((128, 256), 1)
    for f in range(3):
        tail_shift = []
        for e in range(3):
            j = tail_from - 32 * f
            hit = (j >= 0) & (j < 32) & (128 + j == tail_to + e - 1)
            tail_shift.append(jnp.where(hit, 1.0, 0.0).astype(BF16))
        wide = dot(picked[f].reshape(128, 128), shift[0:128]) + dot(
            picked[3].reshape(128, 128), jnp.concatenate(tail_shift, axis=1)
        )
        put_shifted(2 + f, wide)

    arrived(params)
    lane = iota((384, 128), 1)
    lane96 = iota((96, 128), 1)
    sum1[...] = jnp.zeros_like(sum1)
    sum2[...] = jnp.zeros_like(sum2)

    def all_taps():
        return jnp.concatenate([win[i % 2, i // 2] for i in range(8)], axis=0)

    def first_row(t, h):
        window = jnp.concatenate(
            [shifted[t + a, h : h + 3].reshape(144, 256) for a in range(3)], axis=0
        )
        got = dot(all_taps(), window)
        first = got[:, 0:128].astype(BF16)
        x1[t + 2, SLOT_OF[h]] = first
        return first.astype(F32), got[:, 128:256]

    @pl.loop(0, 3)
    def _(t):
        tail = jnp.zeros((384, 128), F32)
        for h in range(1, 5):
            full, ends = first_row(t, h)
            if h > 1:
                ends = pltpu.roll(ends, 32 * (h - 1), 1)
            hit = (lane >= 32 * (h - 1)) & (lane < 32 * h)
            tail = jnp.where(hit, ends, tail)
            sum1[...] += full
            sum2[...] += full * full
        tail = tail.astype(BF16)
        x1[t + 2, TAIL] = tail
        full = tail.astype(F32)
        sum1[...] += full
        sum2[...] += full * full

    def first_rims():
        @pl.loop(0, 3)
        def _(t):
            _, ends = first_row(t, 0)
            x1[t + 2, UP_TAIL] = pltpu.roll(ends, 96, 1).astype(BF16)
            _, ends = first_row(t, 5)
            x1[t + 2, DOWN_TAIL] = ends.astype(BF16)


    channel, group = iota((384, 128), 0), iota((384, 128), 1)

    def member(first_lane):
        low = (group - first_lane) * GSIZE
        hit = (channel >= low) & (channel < low + GSIZE)
        return jnp.where(hit & (group >= first_lane) & (group < first_lane + 32), 1.0, 0.0)

    def stat_row(a, b, rows):
        ones = jnp.ones((8, 128), F32)
        ra = dot_exact(ones, a, ((1,), (1,)))
        rb = dot_exact(ones, b, ((1,), (1,)))
        return ra, rb

    def share_ring(k, peers_):
        mine = stat_ring.at[k, s, core]
        return [remote(mine, mine, ring_peer(i)) for i in peers_]

    def share_plane(k):
        mine = stat.at[k, plane]
        return [remote(mine, mine, plane_peer(i)) for i in range(15)]

    def plane_total(k):
        total = stat[k, 0]
        for i in range(1, 16):
            total = total + stat[k, i]
        return total

    def coefficients(total, column):
        mean = total / entries
        square = pltpu.roll(mean, 96, 1)
        spread_ = jnp.maximum(square - mean * mean, 0.0)
        rstd = lax.rsqrt(spread_ + 1e-06)
        one = member(0)
        mean_c = jnp.sum(one * mean[0:1], axis=1, keepdims=True)
        rstd_c = jnp.sum(one * rstd[0:1], axis=1, keepdims=True)
        mean_ref[...] = jnp.broadcast_to(mean_c, (384, 128))
        eye32 = jnp.where(lane96 == iota((96, 128), 0), 1.0, 0.0)
        gain_c = jnp.concatenate(
            [
                jnp.sum(eye32 * gains[i, column : column + 1], axis=1, keepdims=True)
                for i in range(4)
            ],
            axis=0,
        )
        scale = rstd_c * gain_c * 0.5
        scale_ref[...] = jnp.broadcast_to(scale, (384, 128))

    def prepare(x, t, f, norm):
        no_up = jnp.where(tile == 0, 128, 0)
        no_down = jnp.where(tile == 31, 128, 0)
        down_limit = jnp.where(tile == 31, 32, 0)
        up_limit = jnp.where(tile == 0, 96, 128)

        @pl.loop(0, 4)
        def _(c):
            part = pl.ds(pl.multiple_of(c * 96, 96), 96)
            mean, scale = mean_ref[part], scale_ref[part]

            def act(v):
                v = v.astype(F32)
                if not norm:
                    return v
                u = (v - mean) * scale
                return u + u * jnp.tanh(u)

            if norm:
                for slot in ROW_SLOT:
                    x[f, slot, part] = act(x[f, slot, part]).astype(BF16)
            up = act(x[f, UP_MAIN, part])
            x[f, UP_MAIN, part] = jnp.where(lane96 < no_up, 0.0, up).astype(BF16)
            down = act(x[f, DOWN_MAIN, part])
            x[f, DOWN_MAIN, part] = jnp.where(lane96 < no_down, 0.0, down).astype(BF16)
            mid = act(x[f, TAIL, part])
            rim = jnp.where(
                lane96 < 32,
                x[f, DOWN_TAIL, part].astype(F32),
                x[f, UP_TAIL, part].astype(F32),
            )
            rim = act(rim)
            rim = jnp.where((lane96 < down_limit) | (lane96 >= up_limit), 0.0, rim)
            t[f, 1, part] = mid.astype(BF16)
            t[f, 0, part] = pltpu.roll(jnp.where(lane96 >= 96, rim, mid), 32, 1).astype(BF16)
            t[f, 2, part] = pltpu.roll(jnp.where(lane96 < 32, rim, mid), 96, 1).astype(BF16)

    def conv_step(x, t, w, f, a):
        taps = w[a].reshape(288, 1152)

        def rows(h):
            return jnp.concatenate([x[f, SLOT_OF[h + b]] for b in range(3)], axis=0)

        for p in range(2):
            got = dot(taps, jnp.concatenate([rows(2 * p), rows(2 * p + 1)], axis=1))
            acc[f - a, 2 * p] += got[:, 0:128]
            acc[f - a, 2 * p + 1] += got[:, 128:256]
        acc[f - a, 4] += dot(taps, t[f].reshape(1152, 128))

    def cached_prepare(x, t):
        @pl.loop(0, 2)
        def _(f):
            prepare(x, t, f, False)

    def cached_frames(x, t, w):
        @pl.loop(0, 3)
        def _(i):
            conv_step(x, t, w, jnp.minimum(i, 1), jnp.maximum(i - 1, 0))

    def combined(t):
        def a(i, e):
            return acc[t, i, e * 96 : (e + 1) * 96]

        before = [pltpu.roll(a(h, 0), 1, 1) for h in range(4)]
        mains = []
        for h in range(4):
            after = jnp.where(
                lane96 == 127, pltpu.roll(a(4, 2), 127 - 32 * h, 1), pltpu.roll(a(h, 2), 127, 1)
            )
            mains.append(a(h, 1) + jnp.where(lane96 == 0, 0.0, before[h]) + after)
        left = pltpu.roll(a(4, 0), 1, 1)
        for h in range(4):
            moved = before[h] if h == 0 else pltpu.roll(before[h], 32 * h, 1)
            left = jnp.where(lane96 == 32 * h, moved, left)
        right = jnp.where((lane96 & 31) == 31, 0.0, pltpu.roll(a(4, 2), 127, 1))
        return mains, a(4, 1) + left + right

    ra, rb = stat_row(sum1[...], sum2[...], 384)
    stat_ring[0, s, core] = dot_exact(ra, member(0), ((1,), (0,))) + dot_exact(
        rb, member(32), ((1,), (0,))
    )
    shared = share_ring(0, (3,))
    arrived(shared)
    stat[0, plane] = stat_ring[0, s, 0] + stat_ring[0, s, 1]
    shared = share_plane(0)
    first_rims()
    for t in range(3):
        kept[t] = x1[t + 2, 0:5, own]
    for c in wl1:
        c.wait()
    arrived(rims)
    cached_prepare(x1, t1)
    cached_frames(x1, t1, w1)
    arrived(cached2)
    cached2 = remotes(relay(x2, pl.ds(0, 2)))
    arrived(shared)
    coefficients(plane_total(0), 0)

    sum1[...] = jnp.zeros_like(sum1)
    sum2[...] = jnp.zeros_like(sum2)
    first_copy = taken(36)

    def of_frame(first, moves, t):
        k = first_copy + t * 12 + first
        return [copy_of(k + i, *move) for i, move in enumerate(moves)]

    def middle_spread(t):
        return of_frame(0, spread(x2, t + 2), t)

    def middle_relay(t):
        return of_frame(2, relay(x2, t + 2), t)

    def halo_own(t):
        return of_frame(4, block_halo(x2, t + 2, (0,)), t)

    def halo_near(t):
        return of_frame(6, block_halo(x2, t + 2, (1, 3)), t)

    def halo_far(t):
        return of_frame(10, block_halo(x2, t + 2, (2,)), t)

    def start(copies):
        for c in copies:
            c.start()

    def landed(copies):
        for c in copies:
            c.wait_recv()

    first_rims2 = taken(2)
    rims2 = [copy_of(first_rims2 + i, *m) for i, m in enumerate(halo(x2, pl.ds(0, 2)))]

    @pl.loop(0, 3)
    def _(t):
        prepare(x1, t1, t + 2, True)

        @pl.loop(2 - t, 3)
        def _(a):
            conv_step(x1, t1, w1, t + a, a)

        mains, tail = combined(t)
        acc[t] = jnp.zeros((5, 288, 128), F32)
        total1, total2 = sum1[own], sum2[own]
        for h in range(4):
            x2[t + 2, ROW_SLOT[h], own] = mains[h].astype(BF16)
        x2[t + 2, TAIL, own] = tail.astype(BF16)
        start(middle_spread(t))
        start(halo_own(t))
        for v in mains + [tail]:
            total1 = total1 + v
            total2 = total2 + v * v
        sum1[own] = total1
        sum2[own] = total2

        @pl.when(t == 1)
        def _():
            landed(cached2)
            start(rims2)

    sent.extend(cached2)
    ra, rb = stat_row(sum1[...], sum2[...], 384)
    stat_ring[1, s, core] = dot_exact(ra, member(0), ((1,), (0,))) + dot_exact(
        rb, member(32), ((1,), (0,))
    )
    shared = share_ring(1, range(7))
    landed(middle_spread(0))
    start(middle_relay(0))
    start(halo_near(0))
    for c in wl2:
        c.wait()
    arrived(rims2)
    arrived(shared)
    total = stat_ring[1, 0, 0] + stat_ring[1, 0, 1]
    for i in range(1, 4):
        total = total + (stat_ring[1, i, 0] + stat_ring[1, i, 1])
    stat[1, plane] = total
    shared = share_plane(1)
    landed(middle_spread(1))
    start(middle_relay(1))
    start(halo_near(1))
    cached_prepare(x2, t2)
    landed(middle_relay(0))
    start(halo_far(0))
    landed(middle_spread(2))
    start(middle_relay(2))
    start(halo_near(2))
    cached_frames(x2, t2, w2)
    landed(middle_relay(1))
    start(halo_far(1))
    arrived(shared)
    coefficients(plane_total(1), 1)
    gone()

    @pl.loop(0, 3)
    def _(t):
        edges_ = halo_own(t) + halo_near(t) + halo_far(t)
        landed(edges_)
        for c in middle_spread(t) + middle_relay(t) + edges_:
            c.wait_send()
        prepare(x2, t2, t + 2, True)

        @pl.when(t == 0)
        def _():
            landed(middle_relay(2))
            start(halo_far(2))

        @pl.loop(2 - t, 3)
        def _(a):
            conv_step(x2, t2, w2, t + a, a)

        mains, tail = combined(t)
        for h in range(4):
            out = (kept[t, ROW_SLOT[h]].astype(F32) + mains[h]).astype(BF16)
            out_ref[t, h] = out
        out = (kept[t, TAIL].astype(F32) + tail).astype(BF16)
        out_ref[t, 4] = out


def channels_last(from_ref, to_ref):
    eye = jnp.where(iota((128, 128), 0) == iota((128, 128), 1), 1.0, 0.0).astype(BF16)
    for t in range(3):
        for h in range(4):
            to_ref[t, h, 0:128] = dot_t(eye, from_ref[t, h]).astype(BF16)
        turned = dot_t(eye, from_ref[t, 4]).astype(BF16)
        for h in range(4):
            to_ref[t, h, 128:160] = turned[32 * h : 32 * h + 32]


def per_device(
    latent,
    row_map,
    latent_cache,
    cache_one,
    cache_two,
    conv_in_w,
    weight_one,
    weight_two,
    gain_one,
    gain_two,
):
    frames, _, channels_in, columns = latent.shape
    entries = float(frames * 128 * GSIZE * columns)
    vmem = pl.BlockSpec(memory_space=pltpu.VMEM)
    hbm = pl.BlockSpec(memory_space=pl.ANY)
    copies = 3 + 2 + 7 + 15 + 1 + 3 + 4 + 4 + 2 + 1 + 15 + 36 + 2 + 7 + 15
    decoded = pl.pallas_call(
        functools.partial(body, entries),
        out_shape=jax.ShapeDtypeStruct((3, 5, 96, 128), BF16),
        in_specs=[vmem, vmem, vmem, vmem, vmem, vmem, hbm, hbm, hbm, hbm],
        out_specs=vmem,
        scratch_shapes=[
            pltpu.VMEM((4, 16, 128), BF16),
            pltpu.VMEM((128, 16, 128), BF16),
            pltpu.VMEM((4, 8, 16, 128), BF16),
            pltpu.VMEM((2, 8, 16, 160), BF16),
            pltpu.VMEM((5, 8, 48, 256), BF16),
            pltpu.VMEM((2, 4, 48, 432), BF16),
            pltpu.VMEM((4, 8, 128), F32),
            pltpu.VMEM((128, 2048), BF16),
            pltpu.VMEM((2, 4, 160, 96), BF16),
            pltpu.VMEM((2, 4, 160, 96), BF16),
            pltpu.VMEM((3, 3, 96, 1152), BF16),
            pltpu.VMEM((3, 3, 96, 1152), BF16),
            pltpu.VMEM((5, 9, 384, 128), BF16),
            pltpu.VMEM((5, 9, 384, 128), BF16),
            pltpu.VMEM((5, 3, 384, 128), BF16),
            pltpu.VMEM((5, 3, 384, 128), BF16),
            pltpu.VMEM((3, 5, 288, 128), F32),
            pltpu.VMEM((3, 5, 96, 128), BF16),
            pltpu.VMEM((384, 128), F32),
            pltpu.VMEM((384, 128), F32),
            pltpu.VMEM((384, 128), F32),
            pltpu.VMEM((384, 128), F32),
            pltpu.VMEM((2, 16, 8, 128), F32),
            pltpu.VMEM((2, 4, 2, 8, 128), F32),
            pltpu.SemaphoreType.DMA((copies,)),
            pltpu.SemaphoreType.DMA((copies,)),
            pltpu.SemaphoreType.DMA((8,)),
        ],
        compiler_params=pltpu.CompilerParams(
            collective_id=0, has_side_effects=True, vmem_limit_bytes=56 << 20
        ),
    )(
        row_map.reshape(1, 128),
        latent.reshape(frames, channels_in, columns),
        latent_cache,
        conv_in_w.reshape(27 * channels_in, 96),
        gain_one.reshape(1, 96),
        gain_two.reshape(1, 96),
        jnp.swapaxes(cache_one, 2, 3),
        jnp.swapaxes(cache_two, 2, 3),
        weight_one,
        weight_two,
    )
    decoded = pl.pallas_call(
        channels_last,
        out_shape=jax.ShapeDtypeStruct((3, 4, 160, 96), BF16),
        in_specs=[vmem],
        out_specs=vmem,
    )(decoded)
    return jnp.swapaxes(decoded, 2, 3)


def solution(mesh):
    torus = Mesh(mesh.devices.reshape(SIZES), AXES)
    all_axes = ("src",) + TILE
    in_specs = (
        P(None, all_axes, None, None),
        P(),
        P(None, TILE, None, None),
        P(None, TILE, "src", None),
        P(None, TILE, "src", None),
        P(None, None, None, None, "src"),
        P(None, None, None, "src", None),
        P(None, None, None, "src", None),
        P("src"),
        P("src"),
    )
    return jax.shard_map(
        per_device,
        mesh=torus,
        in_specs=in_specs,
        out_specs=P(None, TILE, "src", None),
        check_vma=False,
    )
```

```python
import functools

import jax
import jax.numpy as jnp
from jax import lax
from jax.experimental import pallas as pl
from jax.experimental.pallas import tpu as pltpu
from jax.sharding import Mesh
from jax.sharding import PartitionSpec as P

GSIZE = 12
GROUPS = 32
AXES = ("src", "z", "y", "core")
TILE = ("z", "y", "core")
SIZES = (4, 4, 4, 2)
MESH = pl.DeviceIdType.MESH
F32 = jnp.float32
BF16 = jnp.bfloat16

TAIL, UP_MAIN, UP_TAIL, DOWN_TAIL, DOWN_MAIN = 3, 5, 6, 7, 8
ROW_SLOT = (4, 0, 1, 2)
SLOT_OF = (UP_MAIN, 4, 0, 1, 2, DOWN_MAIN)
PLANE = tuple((z, y) for z in range(4) for y in range(4) if z or y)


def dot(a, b):
    return lax.dot_general(a, b, (((1,), (0,)), ((), ())), preferred_element_type=F32)


def dot_t(a, b):
    return lax.dot_general(a, b, (((1,), (1,)), ((), ())), preferred_element_type=F32)


def dot_exact(a, b, dims):
    return lax.dot_general(
        a, b, (dims, ((), ())), precision=lax.Precision.HIGHEST, preferred_element_type=F32
    )


def iota(shape, dim):
    return lax.broadcasted_iota(jnp.int32, shape, dim)


def body(
    entries,
    map_ref,
    latent_ref,
    lcache_ref,
    win_ref,
    gain1_ref,
    gain2_ref,
    cache1_hbm,
    cache2_hbm,
    w1_hbm,
    w2_hbm,
    out_ref,
    units,
    rows_all,
    picked,
    lcache,
    shifted,
    win,
    gains,
    choice,
    stage1,
    stage2,
    w1,
    w2,
    x1,
    x2,
    t1,
    t2,
    acc,
    kept,
    sums,
    members,
    gain_cols,
    tail_shifts,
    mean_ref,
    scale_ref,
    stat,
    stat_ring,
    send_sem,
    recv_sem,
    local_sem,
):
    s, z, y, core = (lax.axis_index(a) for a in AXES)
    tile = z * 8 + y * 2 + core
    plane = z * 4 + y
    own = pl.ds(pl.multiple_of(s * 96, 96), 96)
    nxt, prv = lax.rem(tile + 1, 32), lax.rem(tile + 31, 32)

    def at_tile(t):
        return (s, t // 8, lax.rem(t // 2, 4), lax.rem(t, 2))

    def src_peer(d):
        return (lax.rem(s + d, 4), z, y, core)

    def plane_peer(k):
        dz, dy = PLANE[k]
        return (s, lax.rem(z + dz, 4), lax.rem(y + dy, 4), core)

    other = (s, z, y, 1 - core)

    def ring_peer(i):
        if i < 3:
            return src_peer(i + 1)
        return (lax.rem(s + i - 3, 4), z, y, 1 - core)

    counter = [0]

    def taken(count):
        counter[0] += count
        return counter[0] - count

    def copy_of(k, src, dst, device):
        return pltpu.make_async_remote_copy(
            src_ref=src,
            dst_ref=dst,
            send_sem=send_sem.at[k],
            recv_sem=recv_sem.at[k],
            device_id=device,
            device_id_type=MESH,
        )

    def remote(src, dst, device):
        c = copy_of(taken(1), src, dst, device)
        c.start()
        return c

    def remotes(moves):
        return [remote(*move) for move in moves]

    def local(src, dst, k):
        c = pltpu.make_async_copy(src, dst, local_sem.at[k])
        c.start()
        return c

    sent = []

    def arrived(copies):
        for c in copies:
            c.wait_recv()
        sent.extend(copies)

    def gone():
        for c in sent:
            c.wait_send()
        sent.clear()

    barrier = pltpu.get_barrier_semaphore()
    peers = [src_peer(d) for d in (1, 2, 3)] + [plane_peer(k) for k in range(15)]
    peers += [ring_peer(i) for i in range(3, 7)] + [at_tile(nxt), at_tile(prv)]
    for p in peers:
        pl.semaphore_signal(barrier, inc=1, device_id=p, device_id_type=MESH)
    c1 = local(cache1_hbm, stage1, 0)
    c2 = local(cache2_hbm, stage2, 1)
    wl1 = [
        local(w1_hbm.at[:, b], w1.at[:, :, :, pl.ds(b * 384, 384)], 2 + b) for b in range(3)
    ]
    wl2 = [
        local(w2_hbm.at[:, b], w2.at[:, :, :, pl.ds(b * 384, 384)], 5 + b) for b in range(3)
    ]

    from_col, to_col = iota((160, 128), 0), iota((160, 128), 1)

    def tail_place(k):
        hit = (from_col >= 128) & (from_col - 128 == to_col - 32 * k)
        return jnp.where(hit, 1.0, 0.0).astype(BF16)

    place = [tail_place(k) for k in range(3)]

    for f in range(3):
        units[f] = latent_ref[f, :, 0:128]
    tails = sum(dot(latent_ref[f], place[f]) for f in range(3))
    units[3] = tails.astype(BF16)
    base = pl.multiple_of(core * 64 + plane * 4, 4)
    rows_all[base + s] = units[s]
    eye = jnp.where(iota((96, 96), 0) == iota((96, 96), 1), 1.0, 0.0).astype(BF16)
    taps_in = dot_t(eye, win_ref[...]).astype(BF16)
    win[0, s] = taps_in[0:48]
    win[1, s] = taps_in[48:96]
    gains[s] = jnp.zeros((8, 128), F32)
    gains[s, 0:1, 0:96] = gain1_ref[...]
    gains[s, 1:2, 0:96] = gain2_ref[...]
    acc[...] = jnp.zeros_like(acc)
    sum1, sum2 = sums.at[0:384], sums.at[384:768]
    channel, group = iota((384, 128), 0), iota((384, 128), 1)
    for i in range(2):
        low = (group - 32 * i) * GSIZE
        hit = (channel >= low) & (channel < low + GSIZE)
        hit &= (group >= 32 * i) & (group < 32 * i + 32)
        members[384 * i : 384 * i + 384] = jnp.where(hit, 1.0, 0.0)
    sums[...] = jnp.zeros_like(sums)
    for f in range(2):
        lcache[f, 2:6] = lcache_ref[f]
    def pack_cache(staged, x):
        for f in range(2):
            for h in range(4):
                x[f, ROW_SLOT[h], own] = dot_t(eye, staged[f, h, 0:128]).astype(BF16)
            tails = jnp.concatenate([staged[f, h, 128:160] for h in range(4)], axis=0)
            x[f, TAIL, own] = dot_t(eye, tails).astype(BF16)

    c1.wait()
    pack_cache(stage1, x1)
    pl.semaphore_wait(barrier, len(peers))

    step0 = [
        remote(units.at[lax.rem(s + d, 4)], rows_all.at[base + s], src_peer(d)) for d in (1, 2, 3)
    ]
    edges = [
        remote(lcache_ref.at[:, 2:4], lcache.at[:, 0:2], at_tile(nxt)),
        remote(lcache_ref.at[:, 0:2], lcache.at[:, 6:8], at_tile(prv)),
    ]
    params = [remote(gains.at[s], gains.at[s], src_peer(d)) for d in (1, 2, 3)]

    def spread(x, frames):
        block = x.at[frames, 0:5, own]
        return [(block, block, src_peer(d)) for d in (1, 3)]

    def relay(x, frames):
        moves = []
        for d, first in ((1, 0), (3, 48)):
            part = pl.ds(pl.multiple_of(lax.rem(s + 4 - d, 4) * 96 + first, 16), 48)
            block = x.at[frames, 0:5, part]
            moves.append((block, block, src_peer(d)))
        return moves

    def block_halo(x, frames, ways):
        moves = []
        for d in ways:
            part = pl.ds(pl.multiple_of(lax.rem(s + d, 4) * 96, 96), 96)
            moves += [
                (x.at[frames, 2:4, part], x.at[frames, 5:7, part], at_tile(nxt)),
                (x.at[frames, 3:5, part], x.at[frames, 7:9, part], at_tile(prv)),
            ]
        return moves

    cached1 = remotes(spread(x1, pl.ds(0, 2)))
    rims = remotes(block_halo(x1, pl.ds(0, 2), (0,)))
    mine = win.at[core, s]
    params += [remote(mine, mine, src_peer(d)) for d in (1, 2, 3)]
    arrived(step0)
    mine = rows_all.at[pl.ds(base, 4)]
    step1 = [remote(mine, mine, plane_peer(k)) for k in range(15)]
    c2.wait()
    pack_cache(stage2, x2)
    place_of, slot_of = iota((128, 2048), 0), iota((128, 2048), 1) // 16
    held = (lax.rem(slot_of, 4) * 32) + lax.rem(slot_of // 4, 16) * 2 + slot_of // 64
    holds = jnp.where(place_of == held, 1.0, 0.0).astype(BF16)
    image_rows = jnp.broadcast_to(map_ref[...].astype(F32), (8, 128)).astype(BF16)
    row_at = dot(image_rows, holds)[0:1].astype(jnp.int32)
    wanted = jnp.clip(tile * 4 - 2 + iota((128, 2048), 0) // 16, 0, 127)
    same = lax.rem(iota((128, 2048), 0), 16) == lax.rem(iota((128, 2048), 1), 16)
    choice[...] = jnp.where((row_at == wanted) & same, 1.0, 0.0).astype(BF16)

    wide_from, wide_to = iota((160, 256), 0), iota((160, 256), 1)
    shift = jnp.concatenate(
        [jnp.where(wide_from == wide_to + e - 1, 1.0, 0.0).astype(BF16) for e in range(3)], axis=1
    )
    image_row = tile * 4 - 2 + iota((8, 16, 256), 0)
    in_image = (image_row >= 0) & (image_row < 128)

    def put_shifted(f, wide):
        for e in range(3):
            part = wide[:, e * 256 : (e + 1) * 256].reshape(8, 16, 256)
            shifted[f, :, e * 16 : (e + 1) * 16] = jnp.where(in_image, part, 0.0).astype(BF16)

    tail_from, tail_to = iota((128, 256), 0), iota((128, 256), 1)
    for f in range(3):
        for e in range(3):
            j = tail_from - 32 * f
            hit = (j >= 0) & (j < 32) & (128 + j == tail_to + e - 1)
            tail_shifts[f, :, 256 * e : 256 * e + 256] = jnp.where(hit, 1.0, 0.0).astype(BF16)
    arrived(edges)
    for f in range(2):
        put_shifted(f, dot(lcache[f].reshape(128, 160), shift))

    arrived(cached1)
    arrived(step1)
    half = rows_all.at[pl.ds(pl.multiple_of(core * 64, 64), 64)]
    step2 = [remote(half, half, other)]
    cached1 = remotes(relay(x1, pl.ds(0, 2)))
    rims += remotes(block_halo(x1, pl.ds(0, 2), (1, 3)))
    arrived(step2)
    chosen = dot(choice[...], rows_all[...].reshape(2048, 128))
    picked[s] = chosen.astype(BF16).reshape(8, 16, 128)
    step3 = [remote(picked.at[s], picked.at[s], src_peer(d)) for d in (1, 2, 3)]
    arrived(params)
    params = [remote(win.at[core], win.at[core], other)]
    arrived(step3)
    cached2 = remotes(spread(x2, pl.ds(0, 2)))
    rims2 = remotes(block_halo(x2, pl.ds(0, 2), (0,)))
    for f in range(3):
        wide = dot(picked[f].reshape(128, 128), shift[0:128]) + dot(
            picked[3].reshape(128, 128), tail_shifts[f]
        )
        put_shifted(2 + f, wide)
    arrived(cached1)
    rims += remotes(block_halo(x1, pl.ds(0, 2), (2,)))

    arrived(params)
    lane = iota((384, 128), 1)
    lane96 = iota((96, 128), 1)

    def all_taps():
        return jnp.concatenate([win[i % 2, i // 2] for i in range(8)], axis=0)

    def first_row(t, h):
        window = jnp.concatenate(
            [shifted[t + a, h : h + 3].reshape(144, 256) for a in range(3)], axis=0
        )
        got = dot(all_taps(), window)
        first = got[:, 0:128].astype(BF16)
        x1[t + 2, SLOT_OF[h]] = first
        return first.astype(F32), got[:, 128:256]

    @pl.loop(0, 3)
    def _(t):
        tail = jnp.zeros((384, 128), F32)
        for h in range(1, 5):
            full, ends = first_row(t, h)
            if h > 1:
                ends = pltpu.roll(ends, 32 * (h - 1), 1)
            hit = (lane >= 32 * (h - 1)) & (lane < 32 * h)
            tail = jnp.where(hit, ends, tail)
            sum1[...] += full
            sum2[...] += full * full
        tail = tail.astype(BF16)
        x1[t + 2, TAIL] = tail
        full = tail.astype(F32)
        sum1[...] += full
        sum2[...] += full * full

    def first_rims():
        @pl.loop(0, 3)
        def _(t):
            _, ends = first_row(t, 0)
            x1[t + 2, UP_TAIL] = pltpu.roll(ends, 96, 1).astype(BF16)
            _, ends = first_row(t, 5)
            x1[t + 2, DOWN_TAIL] = ends.astype(BF16)


    def group_sums():
        rows = dot_exact(jnp.ones((8, 128), F32), sums[...], ((1,), (1,)))
        return dot_exact(rows, members[...], ((1,), (0,)))

    def share_ring(k, peers_):
        mine = stat_ring.at[k, s, core]
        return [remote(mine, mine, ring_peer(i)) for i in peers_]

    def share_plane(k):
        mine = stat.at[k, plane]
        return [remote(mine, mine, plane_peer(i)) for i in range(15)]

    def plane_total(k):
        total = stat[k, 0]
        for i in range(1, 16):
            total = total + stat[k, i]
        return total

    def coefficients(total, column):
        mean = total / entries
        square = pltpu.roll(mean, 96, 1)
        spread_ = jnp.maximum(square - mean * mean, 0.0)
        rstd = lax.rsqrt(spread_ + 1e-06)
        one = members[0:384]
        mean_c = jnp.sum(one * mean[0:1], axis=1, keepdims=True)
        rstd_c = jnp.sum(one * rstd[0:1], axis=1, keepdims=True)
        mean_ref[...] = jnp.broadcast_to(mean_c, (384, 128))
        scale_ref[...] = jnp.broadcast_to(rstd_c, (384, 128)) * gain_cols[column]

    def gain_columns():
        unit = jnp.where(lane96 == iota((96, 128), 0), 0.5, 0.0)
        for column in range(2):
            for i in range(4):
                col = jnp.sum(unit * gains[i, column : column + 1], axis=1, keepdims=True)
                gain_cols[column, 96 * i : 96 * i + 96] = jnp.broadcast_to(col, (96, 128))

    def prepare(x, t, f, norm):
        no_up = jnp.where(tile == 0, 128, 0)
        no_down = jnp.where(tile == 31, 128, 0)
        down_limit = jnp.where(tile == 31, 32, 0)
        up_limit = jnp.where(tile == 0, 96, 128)

        @pl.loop(0, 4, unroll=True)
        def _(c):
            part = pl.ds(pl.multiple_of(c * 96, 96), 96)
            mean, scale = mean_ref[part], scale_ref[part]

            def act(v):
                v = v.astype(F32)
                if not norm:
                    return v
                u = (v - mean) * scale
                return u + u * jnp.tanh(u)

            if norm:
                for slot in ROW_SLOT:
                    x[f, slot, part] = act(x[f, slot, part]).astype(BF16)
            up = act(x[f, UP_MAIN, part])
            x[f, UP_MAIN, part] = jnp.where(lane96 < no_up, 0.0, up).astype(BF16)
            down = act(x[f, DOWN_MAIN, part])
            x[f, DOWN_MAIN, part] = jnp.where(lane96 < no_down, 0.0, down).astype(BF16)
            mid = act(x[f, TAIL, part])
            rim = jnp.where(
                lane96 < 32,
                x[f, DOWN_TAIL, part].astype(F32),
                x[f, UP_TAIL, part].astype(F32),
            )
            rim = act(rim)
            rim = jnp.where((lane96 < down_limit) | (lane96 >= up_limit), 0.0, rim)
            t[f, 1, part] = mid.astype(BF16)
            t[f, 0, part] = pltpu.roll(jnp.where(lane96 >= 96, rim, mid), 32, 1).astype(BF16)
            t[f, 2, part] = pltpu.roll(jnp.where(lane96 < 32, rim, mid), 96, 1).astype(BF16)

    def conv_step(x, t, w, f, a):
        taps = w[a].reshape(288, 1152)

        def rows(h):
            return jnp.concatenate([x[f, SLOT_OF[h + b]] for b in range(3)], axis=0)

        for p in range(2):
            got = dot(taps, jnp.concatenate([rows(2 * p), rows(2 * p + 1)], axis=1))
            acc[f - a, 2 * p] += got[:, 0:128]
            acc[f - a, 2 * p + 1] += got[:, 128:256]
        acc[f - a, 4] += dot(taps, t[f].reshape(1152, 128))

    def conv_taps(x, t, w, f, low, count):
        taps = w[low : low + count].reshape(count * 288, 1152)

        def rows(h):
            return jnp.concatenate([x[f, SLOT_OF[h + b]] for b in range(3)], axis=0)

        for p in range(3):
            if p < 2:
                got = dot(taps, jnp.concatenate([rows(2 * p), rows(2 * p + 1)], axis=1))
            else:
                got = dot(taps, t[f].reshape(1152, 128))
            for n in range(count):
                part = got[n * 288 : (n + 1) * 288]
                if p < 2:
                    acc[f - low - n, 2 * p] += part[:, 0:128]
                    acc[f - low - n, 2 * p + 1] += part[:, 128:256]
                else:
                    acc[f - low - n, 4] += part

    def cached_prepare(x, t):
        @pl.loop(0, 2)
        def _(f):
            prepare(x, t, f, False)

    def cached_frames(x, t, w):
        @pl.loop(0, 3)
        def _(i):
            conv_step(x, t, w, jnp.minimum(i, 1), jnp.maximum(i - 1, 0))

    def combined(t):
        def a(i, e):
            return acc[t, i, e * 96 : (e + 1) * 96]

        before = [pltpu.roll(a(h, 0), 1, 1) for h in range(4)]
        mains = []
        for h in range(4):
            after = jnp.where(
                lane96 == 127, pltpu.roll(a(4, 2), 127 - 32 * h, 1), pltpu.roll(a(h, 2), 127, 1)
            )
            mains.append(a(h, 1) + jnp.where(lane96 == 0, 0.0, before[h]) + after)
        left = pltpu.roll(a(4, 0), 1, 1)
        for h in range(4):
            moved = before[h] if h == 0 else pltpu.roll(before[h], 32 * h, 1)
            left = jnp.where(lane96 == 32 * h, moved, left)
        right = jnp.where((lane96 & 31) == 31, 0.0, pltpu.roll(a(4, 2), 127, 1))
        return mains, a(4, 1) + left + right

    stat_ring[0, s, core] = group_sums()
    shared = share_ring(0, (3,))
    arrived(shared)
    stat[0, plane] = stat_ring[0, s, 0] + stat_ring[0, s, 1]
    shared = share_plane(0)
    gain_columns()
    first_rims()
    for t in range(3):
        kept[t] = x1[t + 2, 0:5, own]
    for c in wl1:
        c.wait()
    arrived(rims)
    cached_prepare(x1, t1)
    cached_frames(x1, t1, w1)
    arrived(cached2)
    cached2 = remotes(relay(x2, pl.ds(0, 2)))
    rims2 += remotes(block_halo(x2, pl.ds(0, 2), (1, 3)))
    arrived(shared)
    coefficients(plane_total(0), 0)

    sums[...] = jnp.zeros_like(sums)
    first_copy = taken(36)

    def of_frame(first, moves, t):
        k = first_copy + t * 12 + first
        return [copy_of(k + i, *move) for i, move in enumerate(moves)]

    def middle_spread(t):
        return of_frame(0, spread(x2, t + 2), t)

    def middle_relay(t):
        return of_frame(2, relay(x2, t + 2), t)

    def halo_own(t):
        return of_frame(4, block_halo(x2, t + 2, (0,)), t)

    def halo_near(t):
        return of_frame(6, block_halo(x2, t + 2, (1, 3)), t)

    def halo_far(t):
        return of_frame(10, block_halo(x2, t + 2, (2,)), t)

    def start(copies):
        for c in copies:
            c.start()

    def landed(copies):
        for c in copies:
            c.wait_recv()

    first_far2 = taken(2)
    far2 = [
        copy_of(first_far2 + i, *m) for i, m in enumerate(block_halo(x2, pl.ds(0, 2), (2,)))
    ]

    @pl.loop(0, 3)
    def _(t):
        prepare(x1, t1, t + 2, True)

        @pl.loop(2 - t, 3)
        def _(a):
            conv_step(x1, t1, w1, t + a, a)

        mains, tail = combined(t)
        acc[t] = jnp.zeros((5, 288, 128), F32)
        total1, total2 = sum1[own], sum2[own]
        for h in range(4):
            x2[t + 2, ROW_SLOT[h], own] = mains[h].astype(BF16)
        x2[t + 2, TAIL, own] = tail.astype(BF16)
        start(middle_spread(t))
        start(halo_own(t))
        for v in mains + [tail]:
            total1 = total1 + v
            total2 = total2 + v * v
        sum1[own] = total1
        sum2[own] = total2

        @pl.when(t == 1)
        def _():
            landed(cached2)
            start(far2)

    sent.extend(cached2)
    stat_ring[1, s, core] = group_sums()
    shared = share_ring(1, range(7))
    landed(middle_spread(0))
    start(middle_relay(0))
    start(halo_near(0))
    for c in wl2:
        c.wait()
    arrived(rims2 + far2)
    arrived(shared)
    total = stat_ring[1, 0, 0] + stat_ring[1, 0, 1]
    for i in range(1, 4):
        total = total + (stat_ring[1, i, 0] + stat_ring[1, i, 1])
    stat[1, plane] = total
    shared = share_plane(1)
    landed(middle_spread(1))
    start(middle_relay(1))
    start(halo_near(1))
    cached_prepare(x2, t2)
    landed(middle_relay(0))
    start(halo_far(0))
    landed(middle_spread(2))
    start(middle_relay(2))
    start(halo_near(2))
    cached_frames(x2, t2, w2)
    landed(middle_relay(1))
    start(halo_far(1))
    arrived(shared)
    coefficients(plane_total(1), 1)
    gone()

    @pl.loop(0, 3)
    def _(t):
        edges_ = halo_own(t) + halo_near(t) + halo_far(t)
        landed(edges_)
        for c in middle_spread(t) + middle_relay(t) + edges_:
            c.wait_send()
        prepare(x2, t2, t + 2, True)

        @pl.when(t == 0)
        def _():
            landed(middle_relay(2))
            start(halo_far(2))

        @pl.when(t == 0)
        def _():
            conv_taps(x2, t2, w2, 2, 0, 3)

        @pl.when(t == 1)
        def _():
            conv_taps(x2, t2, w2, 3, 1, 2)

        @pl.when(t == 2)
        def _():
            conv_taps(x2, t2, w2, 4, 2, 1)

        mains, tail = combined(t)
        for h in range(4):
            out = (kept[t, ROW_SLOT[h]].astype(F32) + mains[h]).astype(BF16)
            out_ref[t, h] = out
        out = (kept[t, TAIL].astype(F32) + tail).astype(BF16)
        out_ref[t, 4] = out


def channels_last(from_ref, to_ref):
    eye = jnp.where(iota((128, 128), 0) == iota((128, 128), 1), 1.0, 0.0).astype(BF16)
    for t in range(3):
        for h in range(4):
            to_ref[t, h, 0:128] = dot_t(eye, from_ref[t, h]).astype(BF16)
        turned = dot_t(eye, from_ref[t, 4]).astype(BF16)
        for h in range(4):
            to_ref[t, h, 128:160] = turned[32 * h : 32 * h + 32]


def per_device(
    latent,
    row_map,
    latent_cache,
    cache_one,
    cache_two,
    conv_in_w,
    weight_one,
    weight_two,
    gain_one,
    gain_two,
):
    frames, _, channels_in, columns = latent.shape
    entries = float(frames * 128 * GSIZE * columns)
    vmem = pl.BlockSpec(memory_space=pltpu.VMEM)
    hbm = pl.BlockSpec(memory_space=pl.ANY)
    copies = 3 + 2 + 7 + 15 + 1 + 3 + 4 + 4 + 8 + 1 + 15 + 36 + 8 + 7 + 15
    decoded = pl.pallas_call(
        functools.partial(body, entries),
        out_shape=jax.ShapeDtypeStruct((3, 5, 96, 128), BF16),
        in_specs=[vmem, vmem, vmem, vmem, vmem, vmem, hbm, hbm, hbm, hbm],
        out_specs=vmem,
        scratch_shapes=[
            pltpu.VMEM((4, 16, 128), BF16),
            pltpu.VMEM((128, 16, 128), BF16),
            pltpu.VMEM((4, 8, 16, 128), BF16),
            pltpu.VMEM((2, 8, 16, 160), BF16),
            pltpu.VMEM((5, 8, 48, 256), BF16),
            pltpu.VMEM((2, 4, 48, 432), BF16),
            pltpu.VMEM((4, 8, 128), F32),
            pltpu.VMEM((128, 2048), BF16),
            pltpu.VMEM((2, 4, 160, 96), BF16),
            pltpu.VMEM((2, 4, 160, 96), BF16),
            pltpu.VMEM((3, 3, 96, 1152), BF16),
            pltpu.VMEM((3, 3, 96, 1152), BF16),
            pltpu.VMEM((5, 9, 384, 128), BF16),
            pltpu.VMEM((5, 9, 384, 128), BF16),
            pltpu.VMEM((5, 3, 384, 128), BF16),
            pltpu.VMEM((5, 3, 384, 128), BF16),
            pltpu.VMEM((3, 5, 288, 128), F32),
            pltpu.VMEM((3, 5, 96, 128), BF16),
            pltpu.VMEM((768, 128), F32),
            pltpu.VMEM((768, 128), F32),
            pltpu.VMEM((2, 384, 128), F32),
            pltpu.VMEM((3, 128, 768), BF16),
            pltpu.VMEM((384, 128), F32),
            pltpu.VMEM((384, 128), F32),
            pltpu.VMEM((2, 16, 8, 128), F32),
            pltpu.VMEM((2, 4, 2, 8, 128), F32),
            pltpu.SemaphoreType.DMA((copies,)),
            pltpu.SemaphoreType.DMA((copies,)),
            pltpu.SemaphoreType.DMA((8,)),
        ],
        compiler_params=pltpu.CompilerParams(
            collective_id=0, has_side_effects=True, vmem_limit_bytes=56 << 20
        ),
    )(
        row_map.reshape(1, 128),
        latent.reshape(frames, channels_in, columns),
        latent_cache,
        conv_in_w.reshape(27 * channels_in, 96),
        gain_one.reshape(1, 96),
        gain_two.reshape(1, 96),
        jnp.swapaxes(cache_one, 2, 3),
        jnp.swapaxes(cache_two, 2, 3),
        weight_one,
        weight_two,
    )
    decoded = pl.pallas_call(
        channels_last,
        out_shape=jax.ShapeDtypeStruct((3, 4, 160, 96), BF16),
        in_specs=[vmem],
        out_specs=vmem,
    )(decoded)
    return jnp.swapaxes(decoded, 2, 3)


def solution(mesh):
    torus = Mesh(mesh.devices.reshape(SIZES), AXES)
    all_axes = ("src",) + TILE
    in_specs = (
        P(None, all_axes, None, None),
        P(),
        P(None, TILE, None, None),
        P(None, TILE, "src", None),
        P(None, TILE, "src", None),
        P(None, None, None, None, "src"),
        P(None, None, None, "src", None),
        P(None, None, None, "src", None),
        P("src"),
        P("src"),
    )
    return jax.shard_map(
        per_device,
        mesh=torus,
        in_specs=in_specs,
        out_specs=P(None, TILE, "src", None),
        check_vma=False,
    )
```

```python
import functools

import jax
import jax.numpy as jnp
from jax import lax
from jax.experimental import pallas as pl
from jax.experimental.pallas import tpu as pltpu
from jax.sharding import Mesh
from jax.sharding import PartitionSpec as P

GSIZE = 12
GROUPS = 32
AXES = ("src", "z", "y", "core")
TILE = ("z", "y", "core")
SIZES = (4, 4, 4, 2)
MESH = pl.DeviceIdType.MESH
F32 = jnp.float32
BF16 = jnp.bfloat16

TAIL, UP_MAIN, UP_TAIL, DOWN_TAIL, DOWN_MAIN = 3, 5, 6, 7, 8
ROW_SLOT = (4, 0, 1, 2)
SLOT_OF = (UP_MAIN, 4, 0, 1, 2, DOWN_MAIN)
PLANE = tuple(
    sorted(
        ((z, y) for z in range(4) for y in range(4) if z or y),
        key=lambda step: -sum(min(n, 4 - n) for n in step),
    )
)


def dot(a, b):
    return lax.dot_general(a, b, (((1,), (0,)), ((), ())), preferred_element_type=F32)


def dot_t(a, b):
    return lax.dot_general(a, b, (((1,), (1,)), ((), ())), preferred_element_type=F32)


def dot_exact(a, b, dims):
    return lax.dot_general(
        a, b, (dims, ((), ())), precision=lax.Precision.HIGHEST, preferred_element_type=F32
    )


def iota(shape, dim):
    return lax.broadcasted_iota(jnp.int32, shape, dim)


def body(
    entries,
    map_ref,
    latent_ref,
    lcache_ref,
    win_ref,
    gain1_ref,
    gain2_ref,
    cache1_hbm,
    cache2_hbm,
    w1_hbm,
    w2_hbm,
    out_ref,
    units,
    rows_all,
    picked,
    lcache,
    shifted,
    win,
    gains,
    choice,
    stage1,
    stage2,
    w1,
    w2,
    x1,
    x2,
    t1,
    t2,
    acc,
    kept,
    sums,
    members,
    gain_cols,
    tail_shifts,
    mean_ref,
    scale_ref,
    stat,
    stat_ring,
    send_sem,
    recv_sem,
    local_sem,
):
    s, z, y, core = (lax.axis_index(a) for a in AXES)
    tile = z * 8 + y * 2 + core
    plane = z * 4 + y
    own = pl.ds(pl.multiple_of(s * 96, 96), 96)
    nxt, prv = lax.rem(tile + 1, 32), lax.rem(tile + 31, 32)

    def at_tile(t):
        return (s, t // 8, lax.rem(t // 2, 4), lax.rem(t, 2))

    def src_peer(d):
        return (lax.rem(s + d, 4), z, y, core)

    def plane_peer(k):
        dz, dy = PLANE[k]
        return (s, lax.rem(z + dz, 4), lax.rem(y + dy, 4), core)

    other = (s, z, y, 1 - core)

    def ring_peer(i):
        if i < 3:
            return src_peer(i + 1)
        return (lax.rem(s + i - 3, 4), z, y, 1 - core)

    counter = [0]

    def taken(count):
        counter[0] += count
        return counter[0] - count

    def copy_of(k, src, dst, device):
        return pltpu.make_async_remote_copy(
            src_ref=src,
            dst_ref=dst,
            send_sem=send_sem.at[k],
            recv_sem=recv_sem.at[k],
            device_id=device,
            device_id_type=MESH,
        )

    def remote(src, dst, device):
        c = copy_of(taken(1), src, dst, device)
        c.start()
        return c

    def remotes(moves):
        return [remote(*move) for move in moves]

    def local(src, dst, k):
        c = pltpu.make_async_copy(src, dst, local_sem.at[k])
        c.start()
        return c

    sent = []

    def arrived(copies):
        for c in copies:
            c.wait_recv()
        sent.extend(copies)

    def gone():
        for c in sent:
            c.wait_send()
        sent.clear()

    barrier = pltpu.get_barrier_semaphore()
    peers = [plane_peer(k) for k in range(15)] + [src_peer(d) for d in (2, 1, 3)]
    peers += [at_tile(nxt), at_tile(prv)] + [ring_peer(i) for i in (5, 4, 6, 3)]
    for p in peers:
        pl.semaphore_signal(barrier, inc=1, device_id=p, device_id_type=MESH)
    c1 = local(cache1_hbm, stage1, 0)
    c2 = local(cache2_hbm, stage2, 1)
    wl1 = [
        local(w1_hbm.at[:, b], w1.at[:, :, :, pl.ds(b * 384, 384)], 2 + b) for b in range(3)
    ]
    wl2 = [
        local(w2_hbm.at[:, b], w2.at[:, :, :, pl.ds(b * 384, 384)], 5 + b) for b in range(3)
    ]

    from_col, to_col = iota((160, 128), 0), iota((160, 128), 1)

    def tail_place(k):
        hit = (from_col >= 128) & (from_col - 128 == to_col - 32 * k)
        return jnp.where(hit, 1.0, 0.0).astype(BF16)

    place = [tail_place(k) for k in range(3)]

    for f in range(3):
        units[f] = latent_ref[f, :, 0:128]
    tails = sum(dot(latent_ref[f], place[f]) for f in range(3))
    units[3] = tails.astype(BF16)
    base = pl.multiple_of(core * 64 + plane * 4, 4)
    rows_all[base + s] = units[s]
    eye = jnp.where(iota((96, 96), 0) == iota((96, 96), 1), 1.0, 0.0).astype(BF16)
    taps_in = dot_t(eye, win_ref[...]).astype(BF16)
    win[0, s] = taps_in[0:48]
    win[1, s] = taps_in[48:96]
    gains[s] = jnp.zeros((8, 128), F32)
    gains[s, 0:1, 0:96] = gain1_ref[...]
    gains[s, 1:2, 0:96] = gain2_ref[...]
    acc[...] = jnp.zeros_like(acc)
    sum1, sum2 = sums.at[0:384], sums.at[384:768]
    channel, group = iota((384, 128), 0), iota((384, 128), 1)
    for i in range(2):
        low = (group - 32 * i) * GSIZE
        hit = (channel >= low) & (channel < low + GSIZE)
        hit &= (group >= 32 * i) & (group < 32 * i + 32)
        members[384 * i : 384 * i + 384] = jnp.where(hit, 1.0, 0.0)
    sums[...] = jnp.zeros_like(sums)
    for f in range(2):
        lcache[f, 2:6] = lcache_ref[f]
    def pack_cache(staged, x):
        for f in range(2):
            for h in range(4):
                x[f, ROW_SLOT[h], own] = dot_t(eye, staged[f, h, 0:128]).astype(BF16)
            tails = jnp.concatenate([staged[f, h, 128:160] for h in range(4)], axis=0)
            x[f, TAIL, own] = dot_t(eye, tails).astype(BF16)

    c1.wait()
    pack_cache(stage1, x1)
    pl.semaphore_wait(barrier, len(peers))

    step0 = [
        remote(units.at[lax.rem(s + d, 4)], rows_all.at[base + s], src_peer(d)) for d in (2, 1, 3)
    ]
    edges = [
        remote(lcache_ref.at[:, 2:4], lcache.at[:, 0:2], at_tile(nxt)),
        remote(lcache_ref.at[:, 0:2], lcache.at[:, 6:8], at_tile(prv)),
    ]
    params = [remote(gains.at[s], gains.at[s], src_peer(d)) for d in (1, 2, 3)]

    def spread(x, frames):
        block = x.at[frames, 0:5, own]
        return [(block, block, src_peer(d)) for d in (1, 3)]

    def relay(x, frames):
        moves = []
        for d, first in ((1, 0), (3, 48)):
            part = pl.ds(pl.multiple_of(lax.rem(s + 4 - d, 4) * 96 + first, 16), 48)
            block = x.at[frames, 0:5, part]
            moves.append((block, block, src_peer(d)))
        return moves

    def block_halo(x, frames, ways):
        moves = []
        for d in ways:
            part = pl.ds(pl.multiple_of(lax.rem(s + d, 4) * 96, 96), 96)
            moves += [
                (x.at[frames, 2:4, part], x.at[frames, 5:7, part], at_tile(nxt)),
                (x.at[frames, 3:5, part], x.at[frames, 7:9, part], at_tile(prv)),
            ]
        return moves

    cached1 = remotes(spread(x1, pl.ds(0, 2)))
    rims = remotes(block_halo(x1, pl.ds(0, 2), (0,)))
    mine = win.at[core, s]
    params += [remote(mine, mine, src_peer(d)) for d in (1, 2, 3)]
    arrived(step0)
    mine = rows_all.at[pl.ds(base, 4)]
    step1 = [remote(mine, mine, plane_peer(k)) for k in range(15)]
    c2.wait()
    pack_cache(stage2, x2)
    place_of, slot_of = iota((128, 2048), 0), iota((128, 2048), 1) // 16
    held = (lax.rem(slot_of, 4) * 32) + lax.rem(slot_of // 4, 16) * 2 + slot_of // 64
    holds = jnp.where(place_of == held, 1.0, 0.0).astype(BF16)
    image_rows = jnp.broadcast_to(map_ref[...].astype(F32), (8, 128)).astype(BF16)
    row_at = dot(image_rows, holds)[0:1].astype(jnp.int32)
    wanted = jnp.clip(tile * 4 - 2 + iota((128, 2048), 0) // 16, 0, 127)
    same = lax.rem(iota((128, 2048), 0), 16) == lax.rem(iota((128, 2048), 1), 16)
    choice[...] = jnp.where((row_at == wanted) & same, 1.0, 0.0).astype(BF16)

    wide_from, wide_to = iota((160, 256), 0), iota((160, 256), 1)
    shift = jnp.concatenate(
        [jnp.where(wide_from == wide_to + e - 1, 1.0, 0.0).astype(BF16) for e in range(3)], axis=1
    )
    image_row = tile * 4 - 2 + iota((8, 16, 256), 0)
    in_image = (image_row >= 0) & (image_row < 128)

    def put_shifted(f, wide):
        for e in range(3):
            part = wide[:, e * 256 : (e + 1) * 256].reshape(8, 16, 256)
            shifted[f, :, e * 16 : (e + 1) * 16] = jnp.where(in_image, part, 0.0).astype(BF16)

    tail_from, tail_to = iota((128, 256), 0), iota((128, 256), 1)
    for f in range(3):
        for e in range(3):
            j = tail_from - 32 * f
            hit = (j >= 0) & (j < 32) & (128 + j == tail_to + e - 1)
            tail_shifts[f, :, 256 * e : 256 * e + 256] = jnp.where(hit, 1.0, 0.0).astype(BF16)
    arrived(edges)
    for f in range(2):
        put_shifted(f, dot(lcache[f].reshape(128, 160), shift))

    arrived(cached1)
    arrived(step1)
    half = rows_all.at[pl.ds(pl.multiple_of(core * 64, 64), 64)]
    step2 = [remote(half, half, other)]
    cached1 = remotes(relay(x1, pl.ds(0, 2)))
    rims += remotes(block_halo(x1, pl.ds(0, 2), (1, 3)))
    arrived(step2)
    chosen = dot(choice[...], rows_all[...].reshape(2048, 128))
    picked[s] = chosen.astype(BF16).reshape(8, 16, 128)
    step3 = [remote(picked.at[s], picked.at[s], src_peer(d)) for d in (2, 1, 3)]
    arrived(params)
    params = [remote(win.at[core], win.at[core], other)]
    arrived(step3)
    cached2 = remotes(spread(x2, pl.ds(0, 2)))
    rims2 = remotes(block_halo(x2, pl.ds(0, 2), (0,)))
    for f in range(3):
        wide = dot(picked[f].reshape(128, 128), shift[0:128]) + dot(
            picked[3].reshape(128, 128), tail_shifts[f]
        )
        put_shifted(2 + f, wide)
    arrived(cached1)
    rims += remotes(block_halo(x1, pl.ds(0, 2), (2,)))

    arrived(params)
    lane = iota((384, 128), 1)
    lane96 = iota((96, 128), 1)

    def all_taps():
        return jnp.concatenate([win[i % 2, i // 2] for i in range(8)], axis=0)

    def first_row(t, h):
        window = jnp.concatenate(
            [shifted[t + a, h : h + 3].reshape(144, 256) for a in range(3)], axis=0
        )
        got = dot(all_taps(), window)
        first = got[:, 0:128].astype(BF16)
        x1[t + 2, SLOT_OF[h]] = first
        return first.astype(F32), got[:, 128:256]

    @pl.loop(0, 3)
    def _(t):
        tail = jnp.zeros((384, 128), F32)
        for h in range(1, 5):
            full, ends = first_row(t, h)
            if h > 1:
                ends = pltpu.roll(ends, 32 * (h - 1), 1)
            hit = (lane >= 32 * (h - 1)) & (lane < 32 * h)
            tail = jnp.where(hit, ends, tail)
            sum1[...] += full
            sum2[...] += full * full
        tail = tail.astype(BF16)
        x1[t + 2, TAIL] = tail
        full = tail.astype(F32)
        sum1[...] += full
        sum2[...] += full * full

    def first_rims():
        @pl.loop(0, 3)
        def _(t):
            _, ends = first_row(t, 0)
            x1[t + 2, UP_TAIL] = pltpu.roll(ends, 96, 1).astype(BF16)
            _, ends = first_row(t, 5)
            x1[t + 2, DOWN_TAIL] = ends.astype(BF16)


    def group_sums():
        rows = dot_exact(jnp.ones((8, 128), F32), sums[...], ((1,), (1,)))
        return dot_exact(rows, members[...], ((1,), (0,)))

    def share_ring(k, peers_):
        mine = stat_ring.at[k, s, core]
        return [remote(mine, mine, ring_peer(i)) for i in peers_]

    def share_plane(k):
        mine = stat.at[k, plane]
        return [remote(mine, mine, plane_peer(i)) for i in range(15)]

    def plane_total(k):
        total = stat[k, 0]
        for i in range(1, 16):
            total = total + stat[k, i]
        return total

    def coefficients(total, column):
        mean = total / entries
        square = pltpu.roll(mean, 96, 1)
        spread_ = jnp.maximum(square - mean * mean, 0.0)
        rstd = lax.rsqrt(spread_ + 1e-06)
        one = members[0:384]
        mean_c = jnp.sum(one * mean[0:1], axis=1, keepdims=True)
        rstd_c = jnp.sum(one * rstd[0:1], axis=1, keepdims=True)
        mean_ref[...] = jnp.broadcast_to(mean_c, (384, 128))
        scale_ref[...] = jnp.broadcast_to(rstd_c, (384, 128)) * gain_cols[column]

    def gain_columns():
        unit = jnp.where(lane96 == iota((96, 128), 0), 0.5, 0.0)
        for column in range(2):
            for i in range(4):
                col = jnp.sum(unit * gains[i, column : column + 1], axis=1, keepdims=True)
                gain_cols[column, 96 * i : 96 * i + 96] = jnp.broadcast_to(col, (96, 128))

    def prepare(x, t, f, norm):
        no_up = jnp.where(tile == 0, 128, 0)
        no_down = jnp.where(tile == 31, 128, 0)
        down_limit = jnp.where(tile == 31, 32, 0)
        up_limit = jnp.where(tile == 0, 96, 128)

        @pl.loop(0, 4, unroll=True)
        def _(c):
            part = pl.ds(pl.multiple_of(c * 96, 96), 96)
            mean, scale = mean_ref[part], scale_ref[part]

            def act(v):
                v = v.astype(F32)
                if not norm:
                    return v
                u = (v - mean) * scale
                return u + u * jnp.tanh(u)

            if norm:
                for slot in ROW_SLOT:
                    x[f, slot, part] = act(x[f, slot, part]).astype(BF16)
            up = act(x[f, UP_MAIN, part])
            x[f, UP_MAIN, part] = jnp.where(lane96 < no_up, 0.0, up).astype(BF16)
            down = act(x[f, DOWN_MAIN, part])
            x[f, DOWN_MAIN, part] = jnp.where(lane96 < no_down, 0.0, down).astype(BF16)
            mid = act(x[f, TAIL, part])
            rim = jnp.where(
                lane96 < 32,
                x[f, DOWN_TAIL, part].astype(F32),
                x[f, UP_TAIL, part].astype(F32),
            )
            rim = act(rim)
            rim = jnp.where((lane96 < down_limit) | (lane96 >= up_limit), 0.0, rim)
            t[f, 1, part] = mid.astype(BF16)
            t[f, 0, part] = pltpu.roll(jnp.where(lane96 >= 96, rim, mid), 32, 1).astype(BF16)
            t[f, 2, part] = pltpu.roll(jnp.where(lane96 < 32, rim, mid), 96, 1).astype(BF16)

    def conv_step(x, t, w, f, a):
        taps = w[a].reshape(288, 1152)

        def rows(h):
            return jnp.concatenate([x[f, SLOT_OF[h + b]] for b in range(3)], axis=0)

        for p in range(2):
            got = dot(taps, jnp.concatenate([rows(2 * p), rows(2 * p + 1)], axis=1))
            acc[f - a, 2 * p] += got[:, 0:128]
            acc[f - a, 2 * p + 1] += got[:, 128:256]
        acc[f - a, 4] += dot(taps, t[f].reshape(1152, 128))

    def conv_taps(x, t, w, f, low, count):
        taps = w[low : low + count].reshape(count * 288, 1152)

        def rows(h):
            return jnp.concatenate([x[f, SLOT_OF[h + b]] for b in range(3)], axis=0)

        for p in range(3):
            if p < 2:
                got = dot(taps, jnp.concatenate([rows(2 * p), rows(2 * p + 1)], axis=1))
            else:
                got = dot(taps, t[f].reshape(1152, 128))
            for n in range(count):
                part = got[n * 288 : (n + 1) * 288]
                if p < 2:
                    acc[f - low - n, 2 * p] += part[:, 0:128]
                    acc[f - low - n, 2 * p + 1] += part[:, 128:256]
                else:
                    acc[f - low - n, 4] += part

    def cached_prepare(x, t):
        @pl.loop(0, 2)
        def _(f):
            prepare(x, t, f, False)

    def cached_frames(x, t, w):
        @pl.loop(0, 3)
        def _(i):
            conv_step(x, t, w, jnp.minimum(i, 1), jnp.maximum(i - 1, 0))

    def combined(t):
        def a(i, e):
            return acc[t, i, e * 96 : (e + 1) * 96]

        before = [pltpu.roll(a(h, 0), 1, 1) for h in range(4)]
        mains = []
        for h in range(4):
            after = jnp.where(
                lane96 == 127, pltpu.roll(a(4, 2), 127 - 32 * h, 1), pltpu.roll(a(h, 2), 127, 1)
            )
            mains.append(a(h, 1) + jnp.where(lane96 == 0, 0.0, before[h]) + after)
        left = pltpu.roll(a(4, 0), 1, 1)
        for h in range(4):
            moved = before[h] if h == 0 else pltpu.roll(before[h], 32 * h, 1)
            left = jnp.where(lane96 == 32 * h, moved, left)
        right = jnp.where((lane96 & 31) == 31, 0.0, pltpu.roll(a(4, 2), 127, 1))
        return mains, a(4, 1) + left + right

    stat_ring[0, s, core] = group_sums()
    shared = share_ring(0, (3,))
    arrived(shared)
    stat[0, plane] = stat_ring[0, s, 0] + stat_ring[0, s, 1]
    shared = share_plane(0)
    gain_columns()
    first_rims()
    for t in range(3):
        kept[t] = x1[t + 2, 0:5, own]
    for c in wl1:
        c.wait()
    arrived(rims)
    cached_prepare(x1, t1)
    cached_frames(x1, t1, w1)
    arrived(cached2)
    cached2 = remotes(relay(x2, pl.ds(0, 2)))
    rims2 += remotes(block_halo(x2, pl.ds(0, 2), (1, 3)))
    arrived(shared)
    coefficients(plane_total(0), 0)

    sums[...] = jnp.zeros_like(sums)
    first_copy = taken(36)

    def of_frame(first, moves, t):
        k = first_copy + t * 12 + first
        return [copy_of(k + i, *move) for i, move in enumerate(moves)]

    def middle_spread(t):
        return of_frame(0, spread(x2, t + 2), t)

    def middle_relay(t):
        return of_frame(2, relay(x2, t + 2), t)

    def halo_own(t):
        return of_frame(4, block_halo(x2, t + 2, (0,)), t)

    def halo_near(t):
        return of_frame(6, block_halo(x2, t + 2, (1, 3)), t)

    def halo_far(t):
        return of_frame(10, block_halo(x2, t + 2, (2,)), t)

    def start(copies):
        for c in copies:
            c.start()

    def landed(copies):
        for c in copies:
            c.wait_recv()

    first_far2 = taken(2)
    far2 = [
        copy_of(first_far2 + i, *m) for i, m in enumerate(block_halo(x2, pl.ds(0, 2), (2,)))
    ]

    @pl.loop(0, 3)
    def _(t):
        prepare(x1, t1, t + 2, True)

        @pl.loop(2 - t, 3)
        def _(a):
            conv_step(x1, t1, w1, t + a, a)

        mains, tail = combined(t)
        acc[t] = jnp.zeros((5, 288, 128), F32)
        total1, total2 = sum1[own], sum2[own]
        for h in range(4):
            x2[t + 2, ROW_SLOT[h], own] = mains[h].astype(BF16)
        x2[t + 2, TAIL, own] = tail.astype(BF16)
        start(middle_spread(t))
        start(halo_own(t))
        for v in mains + [tail]:
            total1 = total1 + v
            total2 = total2 + v * v
        sum1[own] = total1
        sum2[own] = total2

        @pl.when(t == 1)
        def _():
            landed(cached2)
            start(far2)

    sent.extend(cached2)
    stat_ring[1, s, core] = group_sums()
    shared = share_ring(1, (5, 1, 4, 6, 0, 2, 3))
    landed(middle_spread(0))
    start(middle_relay(0))
    start(halo_near(0))
    for c in wl2:
        c.wait()
    arrived(rims2 + far2)
    arrived(shared)
    total = stat_ring[1, 0, 0] + stat_ring[1, 0, 1]
    for i in range(1, 4):
        total = total + (stat_ring[1, i, 0] + stat_ring[1, i, 1])
    stat[1, plane] = total
    shared = share_plane(1)
    landed(middle_spread(1))
    start(middle_relay(1))
    start(halo_near(1))
    cached_prepare(x2, t2)
    landed(middle_relay(0))
    start(halo_far(0))
    landed(middle_spread(2))
    start(middle_relay(2))
    start(halo_near(2))
    cached_frames(x2, t2, w2)
    landed(middle_relay(1))
    start(halo_far(1))
    arrived(shared)
    coefficients(plane_total(1), 1)
    gone()

    @pl.loop(0, 3)
    def _(t):
        edges_ = halo_own(t) + halo_near(t) + halo_far(t)
        landed(edges_)
        for c in middle_spread(t) + middle_relay(t) + edges_:
            c.wait_send()
        prepare(x2, t2, t + 2, True)

        @pl.when(t == 0)
        def _():
            landed(middle_relay(2))
            start(halo_far(2))

        @pl.when(t == 0)
        def _():
            conv_taps(x2, t2, w2, 2, 0, 3)

        @pl.when(t == 1)
        def _():
            conv_taps(x2, t2, w2, 3, 1, 2)

        @pl.when(t == 2)
        def _():
            conv_taps(x2, t2, w2, 4, 2, 1)

        mains, tail = combined(t)
        for h in range(4):
            out = (kept[t, ROW_SLOT[h]].astype(F32) + mains[h]).astype(BF16)
            out_ref[t, h] = out
        out = (kept[t, TAIL].astype(F32) + tail).astype(BF16)
        out_ref[t, 4] = out


def channels_last(from_ref, to_ref):
    eye = jnp.where(iota((128, 128), 0) == iota((128, 128), 1), 1.0, 0.0).astype(BF16)
    for t in range(3):
        for h in range(4):
            to_ref[t, h, 0:128] = dot_t(eye, from_ref[t, h]).astype(BF16)
        turned = dot_t(eye, from_ref[t, 4]).astype(BF16)
        for h in range(4):
            to_ref[t, h, 128:160] = turned[32 * h : 32 * h + 32]


def per_device(
    latent,
    row_map,
    latent_cache,
    cache_one,
    cache_two,
    conv_in_w,
    weight_one,
    weight_two,
    gain_one,
    gain_two,
):
    frames, _, channels_in, columns = latent.shape
    entries = float(frames * 128 * GSIZE * columns)
    vmem = pl.BlockSpec(memory_space=pltpu.VMEM)
    hbm = pl.BlockSpec(memory_space=pl.ANY)
    copies = 3 + 2 + 7 + 15 + 1 + 3 + 4 + 4 + 8 + 1 + 15 + 36 + 8 + 7 + 15
    decoded = pl.pallas_call(
        functools.partial(body, entries),
        out_shape=jax.ShapeDtypeStruct((3, 5, 96, 128), BF16),
        in_specs=[vmem, vmem, vmem, vmem, vmem, vmem, hbm, hbm, hbm, hbm],
        out_specs=vmem,
        scratch_shapes=[
            pltpu.VMEM((4, 16, 128), BF16),
            pltpu.VMEM((128, 16, 128), BF16),
            pltpu.VMEM((4, 8, 16, 128), BF16),
            pltpu.VMEM((2, 8, 16, 160), BF16),
            pltpu.VMEM((5, 8, 48, 256), BF16),
            pltpu.VMEM((2, 4, 48, 432), BF16),
            pltpu.VMEM((4, 8, 128), F32),
            pltpu.VMEM((128, 2048), BF16),
            pltpu.VMEM((2, 4, 160, 96), BF16),
            pltpu.VMEM((2, 4, 160, 96), BF16),
            pltpu.VMEM((3, 3, 96, 1152), BF16),
            pltpu.VMEM((3, 3, 96, 1152), BF16),
            pltpu.VMEM((5, 9, 384, 128), BF16),
            pltpu.VMEM((5, 9, 384, 128), BF16),
            pltpu.VMEM((5, 3, 384, 128), BF16),
            pltpu.VMEM((5, 3, 384, 128), BF16),
            pltpu.VMEM((3, 5, 288, 128), F32),
            pltpu.VMEM((3, 5, 96, 128), BF16),
            pltpu.VMEM((768, 128), F32),
            pltpu.VMEM((768, 128), F32),
            pltpu.VMEM((2, 384, 128), F32),
            pltpu.VMEM((3, 128, 768), BF16),
            pltpu.VMEM((384, 128), F32),
            pltpu.VMEM((384, 128), F32),
            pltpu.VMEM((2, 16, 8, 128), F32),
            pltpu.VMEM((2, 4, 2, 8, 128), F32),
            pltpu.SemaphoreType.DMA((copies,)),
            pltpu.SemaphoreType.DMA((copies,)),
            pltpu.SemaphoreType.DMA((8,)),
        ],
        compiler_params=pltpu.CompilerParams(
            collective_id=0, has_side_effects=True, vmem_limit_bytes=56 << 20
        ),
    )(
        row_map.reshape(1, 128),
        latent.reshape(frames, channels_in, columns),
        latent_cache,
        conv_in_w.reshape(27 * channels_in, 96),
        gain_one.reshape(1, 96),
        gain_two.reshape(1, 96),
        jnp.swapaxes(cache_one, 2, 3),
        jnp.swapaxes(cache_two, 2, 3),
        weight_one,
        weight_two,
    )
    decoded = pl.pallas_call(
        channels_last,
        out_shape=jax.ShapeDtypeStruct((3, 4, 160, 96), BF16),
        in_specs=[vmem],
        out_specs=vmem,
    )(decoded)
    return jnp.swapaxes(decoded, 2, 3)


def solution(mesh):
    torus = Mesh(mesh.devices.reshape(SIZES), AXES)
    all_axes = ("src",) + TILE
    in_specs = (
        P(None, all_axes, None, None),
        P(),
        P(None, TILE, None, None),
        P(None, TILE, "src", None),
        P(None, TILE, "src", None),
        P(None, None, None, None, "src"),
        P(None, None, None, "src", None),
        P(None, None, None, "src", None),
        P("src"),
        P("src"),
    )
    return jax.shard_map(
        per_device,
        mesh=torus,
        in_specs=in_specs,
        out_specs=P(None, TILE, "src", None),
        check_vma=False,
    )
```

```python
import functools

import jax
import jax.numpy as jnp
from jax import lax
from jax.experimental import pallas as pl
from jax.experimental.pallas import tpu as pltpu
from jax.sharding import Mesh
from jax.sharding import PartitionSpec as P

GSIZE = 12
GROUPS = 32
AXES = ("src", "z", "y", "core")
TILE = ("z", "y", "core")
SIZES = (4, 4, 4, 2)
MESH = pl.DeviceIdType.MESH
F32 = jnp.float32
BF16 = jnp.bfloat16

TAIL, UP_MAIN, UP_TAIL, DOWN_TAIL, DOWN_MAIN = 3, 5, 6, 7, 8
ROW_SLOT = (4, 0, 1, 2)
SLOT_OF = (UP_MAIN, 4, 0, 1, 2, DOWN_MAIN)
PLANE = tuple(
    sorted(
        ((z, y) for z in range(4) for y in range(4) if z or y),
        key=lambda step: -sum(min(n, 4 - n) for n in step),
    )
)


def dot(a, b):
    return lax.dot_general(a, b, (((1,), (0,)), ((), ())), preferred_element_type=F32)


def dot_t(a, b):
    return lax.dot_general(a, b, (((1,), (1,)), ((), ())), preferred_element_type=F32)


def dot_exact(a, b, dims):
    return lax.dot_general(
        a, b, (dims, ((), ())), precision=lax.Precision.HIGHEST, preferred_element_type=F32
    )


def iota(shape, dim):
    return lax.broadcasted_iota(jnp.int32, shape, dim)


def body(
    entries,
    map_ref,
    latent_ref,
    lcache_ref,
    win_ref,
    gain1_ref,
    gain2_ref,
    cache1_hbm,
    cache2_hbm,
    w1_hbm,
    w2_hbm,
    out_ref,
    units,
    rows_all,
    picked,
    lcache,
    shifted,
    win,
    gains,
    choice,
    stage1,
    stage2,
    w1,
    w2,
    x1,
    x2,
    t1,
    t2,
    acc,
    kept,
    sums,
    members,
    gain_cols,
    tail_shifts,
    mean_ref,
    scale_ref,
    stat,
    stat_ring,
    send_sem,
    recv_sem,
    local_sem,
):
    s, z, y, core = (lax.axis_index(a) for a in AXES)
    tile = z * 8 + y * 2 + core
    plane = z * 4 + y
    own = pl.ds(pl.multiple_of(s * 96, 96), 96)
    nxt, prv = lax.rem(tile + 1, 32), lax.rem(tile + 31, 32)

    def at_tile(t):
        return (s, t // 8, lax.rem(t // 2, 4), lax.rem(t, 2))

    def src_peer(d):
        return (lax.rem(s + d, 4), z, y, core)

    def plane_peer(k):
        dz, dy = PLANE[k]
        return (s, lax.rem(z + dz, 4), lax.rem(y + dy, 4), core)

    other = (s, z, y, 1 - core)

    def ring_peer(i):
        if i < 3:
            return src_peer(i + 1)
        return (lax.rem(s + i - 3, 4), z, y, 1 - core)

    counter = [0]

    def taken(count):
        counter[0] += count
        return counter[0] - count

    def copy_of(k, src, dst, device):
        return pltpu.make_async_remote_copy(
            src_ref=src,
            dst_ref=dst,
            send_sem=send_sem.at[k],
            recv_sem=recv_sem.at[k],
            device_id=device,
            device_id_type=MESH,
        )

    def remote(src, dst, device):
        c = copy_of(taken(1), src, dst, device)
        c.start()
        return c

    def remotes(moves):
        return [remote(*move) for move in moves]

    def local(src, dst, k):
        c = pltpu.make_async_copy(src, dst, local_sem.at[k])
        c.start()
        return c

    sent = []

    def arrived(copies):
        for c in copies:
            c.wait_recv()
        sent.extend(copies)

    def gone():
        for c in sent:
            c.wait_send()
        sent.clear()

    barrier = pltpu.get_barrier_semaphore()
    peers = [plane_peer(k) for k in range(15)] + [src_peer(d) for d in (2, 1, 3)]
    peers += [at_tile(nxt), at_tile(prv)] + [ring_peer(i) for i in (5, 4, 6, 3)]
    for p in peers:
        pl.semaphore_signal(barrier, inc=1, device_id=p, device_id_type=MESH)
    c1 = local(cache1_hbm, stage1, 0)
    c2 = local(cache2_hbm, stage2, 1)
    wl1 = [
        local(w1_hbm.at[:, b], w1.at[:, :, :, pl.ds(b * 384, 384)], 2 + b) for b in range(3)
    ]
    wl2 = [
        local(w2_hbm.at[:, b], w2.at[:, :, :, pl.ds(b * 384, 384)], 5 + b) for b in range(3)
    ]

    from_col, to_col = iota((160, 128), 0), iota((160, 128), 1)

    def tail_place(k):
        hit = (from_col >= 128) & (from_col - 128 == to_col - 32 * k)
        return jnp.where(hit, 1.0, 0.0).astype(BF16)

    place = [tail_place(k) for k in range(3)]

    for f in range(3):
        units[f] = latent_ref[f, :, 0:128]
    tails = sum(dot(latent_ref[f], place[f]) for f in range(3))
    units[3] = tails.astype(BF16)
    base = pl.multiple_of(core * 64 + plane * 4, 4)
    rows_all[base + s] = units[s]
    eye = jnp.where(iota((96, 96), 0) == iota((96, 96), 1), 1.0, 0.0).astype(BF16)
    taps_in = dot_t(eye, win_ref[...]).astype(BF16)
    win[0, s] = taps_in[0:48]
    win[1, s] = taps_in[48:96]
    gains[s] = jnp.zeros((8, 128), F32)
    gains[s, 0:1, 0:96] = gain1_ref[...]
    gains[s, 1:2, 0:96] = gain2_ref[...]
    acc[...] = jnp.zeros_like(acc)
    sum1, sum2 = sums.at[0:384], sums.at[384:768]
    channel, group = iota((384, 128), 0), iota((384, 128), 1)
    for i in range(2):
        low = (group - 32 * i) * GSIZE
        hit = (channel >= low) & (channel < low + GSIZE)
        hit &= (group >= 32 * i) & (group < 32 * i + 32)
        members[384 * i : 384 * i + 384] = jnp.where(hit, 1.0, 0.0)
    sums[...] = jnp.zeros_like(sums)
    for f in range(2):
        lcache[f, 2:6] = lcache_ref[f]
    def pack_cache(staged, x):
        for f in range(2):
            for h in range(4):
                x[f, ROW_SLOT[h], own] = dot_t(eye, staged[f, h, 0:128]).astype(BF16)
            tails = jnp.concatenate([staged[f, h, 128:160] for h in range(4)], axis=0)
            x[f, TAIL, own] = dot_t(eye, tails).astype(BF16)

    c1.wait()
    pack_cache(stage1, x1)
    pl.semaphore_wait(barrier, len(peers))

    step0 = [
        remote(units.at[lax.rem(s + d, 4)], rows_all.at[base + s], src_peer(d)) for d in (2, 1, 3)
    ]
    edges = [
        remote(lcache_ref.at[:, 2:4], lcache.at[:, 0:2], at_tile(nxt)),
        remote(lcache_ref.at[:, 0:2], lcache.at[:, 6:8], at_tile(prv)),
    ]
    params = [remote(gains.at[s], gains.at[s], src_peer(d)) for d in (1, 2, 3)]

    def spread(x, frames):
        block = x.at[frames, 0:5, own]
        return [(block, block, src_peer(d)) for d in (1, 3)]

    def relay(x, frames):
        moves = []
        for d, first in ((1, 0), (3, 48)):
            part = pl.ds(pl.multiple_of(lax.rem(s + 4 - d, 4) * 96 + first, 16), 48)
            block = x.at[frames, 0:5, part]
            moves.append((block, block, src_peer(d)))
        return moves

    def block_halo(x, frames, ways):
        moves = []
        for d in ways:
            part = pl.ds(pl.multiple_of(lax.rem(s + d, 4) * 96, 96), 96)
            moves += [
                (x.at[frames, 2:4, part], x.at[frames, 5:7, part], at_tile(nxt)),
                (x.at[frames, 3:5, part], x.at[frames, 7:9, part], at_tile(prv)),
            ]
        return moves

    cached1 = remotes(spread(x1, pl.ds(0, 2)))
    rims = remotes(block_halo(x1, pl.ds(0, 2), (0,)))
    mine = win.at[core, s]
    params += [remote(mine, mine, src_peer(d)) for d in (1, 2, 3)]
    arrived(step0)
    mine = rows_all.at[pl.ds(base, 4)]
    step1 = [remote(mine, mine, plane_peer(k)) for k in range(15)]
    c2.wait()
    pack_cache(stage2, x2)
    place_of, slot_of = iota((128, 2048), 0), iota((128, 2048), 1) // 16
    held = (lax.rem(slot_of, 4) * 32) + lax.rem(slot_of // 4, 16) * 2 + slot_of // 64
    holds = jnp.where(place_of == held, 1.0, 0.0).astype(BF16)
    image_rows = jnp.broadcast_to(map_ref[...].astype(F32), (8, 128)).astype(BF16)
    row_at = dot(image_rows, holds)[0:1].astype(jnp.int32)
    wanted = jnp.clip(tile * 4 - 2 + iota((128, 2048), 0) // 16, 0, 127)
    same = lax.rem(iota((128, 2048), 0), 16) == lax.rem(iota((128, 2048), 1), 16)
    choice[...] = jnp.where((row_at == wanted) & same, 1.0, 0.0).astype(BF16)

    wide_from, wide_to = iota((160, 256), 0), iota((160, 256), 1)
    shift = jnp.concatenate(
        [jnp.where(wide_from == wide_to + e - 1, 1.0, 0.0).astype(BF16) for e in range(3)], axis=1
    )
    image_row = tile * 4 - 2 + iota((8, 16, 256), 0)
    in_image = (image_row >= 0) & (image_row < 128)

    def put_shifted(f, wide):
        for e in range(3):
            part = wide[:, e * 256 : (e + 1) * 256].reshape(8, 16, 256)
            shifted[f, :, e * 16 : (e + 1) * 16] = jnp.where(in_image, part, 0.0).astype(BF16)

    tail_from, tail_to = iota((128, 256), 0), iota((128, 256), 1)
    for f in range(3):
        for e in range(3):
            j = tail_from - 32 * f
            hit = (j >= 0) & (j < 32) & (128 + j == tail_to + e - 1)
            tail_shifts[f, :, 256 * e : 256 * e + 256] = jnp.where(hit, 1.0, 0.0).astype(BF16)
    arrived(edges)
    for f in range(2):
        put_shifted(f, dot(lcache[f].reshape(128, 160), shift))

    arrived(cached1)
    arrived(step1)
    half = rows_all.at[pl.ds(pl.multiple_of(core * 64, 64), 64)]
    step2 = [remote(half, half, other)]
    cached1 = remotes(relay(x1, pl.ds(0, 2)))
    rims += remotes(block_halo(x1, pl.ds(0, 2), (1, 3)))
    arrived(step2)
    chosen = dot(choice[...], rows_all[...].reshape(2048, 128))
    picked[s] = chosen.astype(BF16).reshape(8, 16, 128)
    step3 = [remote(picked.at[s], picked.at[s], src_peer(d)) for d in (2, 1, 3)]
    arrived(params)
    params = [remote(win.at[core], win.at[core], other)]
    arrived(step3)
    cached2 = remotes(spread(x2, pl.ds(0, 2)))
    rims2 = remotes(block_halo(x2, pl.ds(0, 2), (0,)))
    for f in range(3):
        wide = dot(picked[f].reshape(128, 128), shift[0:128]) + dot(
            picked[3].reshape(128, 128), tail_shifts[f]
        )
        put_shifted(2 + f, wide)
    arrived(cached1)
    rims += remotes(block_halo(x1, pl.ds(0, 2), (2,)))

    arrived(params)
    lane = iota((384, 128), 1)
    lane96 = iota((96, 128), 1)

    def all_taps():
        return jnp.concatenate([win[i % 2, i // 2] for i in range(8)], axis=0)

    def first_row(t, h):
        window = jnp.concatenate(
            [shifted[t + a, h : h + 3].reshape(144, 256) for a in range(3)], axis=0
        )
        got = dot(all_taps(), window)
        first = got[:, 0:128].astype(BF16)
        x1[t + 2, SLOT_OF[h]] = first
        return first.astype(F32), got[:, 128:256]

    @pl.loop(0, 3)
    def _(t):
        tail = jnp.zeros((384, 128), F32)
        for h in range(1, 5):
            full, ends = first_row(t, h)
            if h > 1:
                ends = pltpu.roll(ends, 32 * (h - 1), 1)
            hit = (lane >= 32 * (h - 1)) & (lane < 32 * h)
            tail = jnp.where(hit, ends, tail)
            sum1[...] += full
            sum2[...] += full * full
        tail = tail.astype(BF16)
        x1[t + 2, TAIL] = tail
        full = tail.astype(F32)
        sum1[...] += full
        sum2[...] += full * full

    def first_rims():
        @pl.loop(0, 3)
        def _(t):
            _, ends = first_row(t, 0)
            x1[t + 2, UP_TAIL] = pltpu.roll(ends, 96, 1).astype(BF16)
            _, ends = first_row(t, 5)
            x1[t + 2, DOWN_TAIL] = ends.astype(BF16)


    def group_sums():
        rows = dot_exact(jnp.ones((8, 128), F32), sums[...], ((1,), (1,)))
        return dot_exact(rows, members[...], ((1,), (0,)))

    def share_ring(k, peers_):
        mine = stat_ring.at[k, s, core]
        return [remote(mine, mine, ring_peer(i)) for i in peers_]

    def share_plane(k):
        mine = stat.at[k, plane]
        return [remote(mine, mine, plane_peer(i)) for i in range(15)]

    def plane_total(k):
        total = stat[k, 0]
        for i in range(1, 16):
            total = total + stat[k, i]
        return total

    def coefficients(total, column):
        mean = total / entries
        square = pltpu.roll(mean, 96, 1)
        spread_ = jnp.maximum(square - mean * mean, 0.0)
        rstd = lax.rsqrt(spread_ + 1e-06)
        one = members[0:384]
        mean_c = jnp.sum(one * mean[0:1], axis=1, keepdims=True)
        rstd_c = jnp.sum(one * rstd[0:1], axis=1, keepdims=True)
        mean_ref[...] = jnp.broadcast_to(mean_c, (384, 128))
        scale_ref[...] = jnp.broadcast_to(rstd_c, (384, 128)) * gain_cols[column]

    def gain_columns():
        unit = jnp.where(lane96 == iota((96, 128), 0), 0.5, 0.0)
        for column in range(2):
            for i in range(4):
                col = jnp.sum(unit * gains[i, column : column + 1], axis=1, keepdims=True)
                gain_cols[column, 96 * i : 96 * i + 96] = jnp.broadcast_to(col, (96, 128))

    def prepare(x, t, f, norm):
        no_up = jnp.where(tile == 0, 128, 0)
        no_down = jnp.where(tile == 31, 128, 0)
        down_limit = jnp.where(tile == 31, 32, 0)
        up_limit = jnp.where(tile == 0, 96, 128)

        @pl.loop(0, 4, unroll=True)
        def _(c):
            part = pl.ds(pl.multiple_of(c * 96, 96), 96)
            mean, scale = mean_ref[part], scale_ref[part]

            def act(v):
                v = v.astype(F32)
                if not norm:
                    return v
                u = (v - mean) * scale
                return u + u * jnp.tanh(u)

            if norm:
                for slot in ROW_SLOT:
                    x[f, slot, part] = act(x[f, slot, part]).astype(BF16)
            up = act(x[f, UP_MAIN, part])
            x[f, UP_MAIN, part] = jnp.where(lane96 < no_up, 0.0, up).astype(BF16)
            down = act(x[f, DOWN_MAIN, part])
            x[f, DOWN_MAIN, part] = jnp.where(lane96 < no_down, 0.0, down).astype(BF16)
            mid = act(x[f, TAIL, part])
            rim = jnp.where(
                lane96 < 32,
                x[f, DOWN_TAIL, part].astype(F32),
                x[f, UP_TAIL, part].astype(F32),
            )
            rim = act(rim)
            rim = jnp.where((lane96 < down_limit) | (lane96 >= up_limit), 0.0, rim)
            t[f, 1, part] = mid.astype(BF16)
            t[f, 0, part] = pltpu.roll(jnp.where(lane96 >= 96, rim, mid), 32, 1).astype(BF16)
            t[f, 2, part] = pltpu.roll(jnp.where(lane96 < 32, rim, mid), 96, 1).astype(BF16)

    def conv_step(x, t, w, f, a):
        taps = w[a].reshape(288, 1152)

        def rows(h):
            return jnp.concatenate([x[f, SLOT_OF[h + b]] for b in range(3)], axis=0)

        for p in range(2):
            got = dot(taps, jnp.concatenate([rows(2 * p), rows(2 * p + 1)], axis=1))
            acc[f - a, 2 * p] += got[:, 0:128]
            acc[f - a, 2 * p + 1] += got[:, 128:256]
        acc[f - a, 4] += dot(taps, t[f].reshape(1152, 128))

    def conv_taps(x, t, w, f, low, count):
        taps = w[low : low + count].reshape(count * 288, 1152)

        def rows(h):
            return jnp.concatenate([x[f, SLOT_OF[h + b]] for b in range(3)], axis=0)

        for p in range(3):
            if p < 2:
                got = dot(taps, jnp.concatenate([rows(2 * p), rows(2 * p + 1)], axis=1))
            else:
                got = dot(taps, t[f].reshape(1152, 128))
            for n in range(count):
                part = got[n * 288 : (n + 1) * 288]
                if p < 2:
                    acc[f - low - n, 2 * p] += part[:, 0:128]
                    acc[f - low - n, 2 * p + 1] += part[:, 128:256]
                else:
                    acc[f - low - n, 4] += part

    def cached_prepare(x, t):
        @pl.loop(0, 2)
        def _(f):
            prepare(x, t, f, False)

    def cached_frames(x, t, w):
        @pl.loop(0, 3)
        def _(i):
            conv_step(x, t, w, jnp.minimum(i, 1), jnp.maximum(i - 1, 0))

    def combined(t):
        def a(i, e):
            return acc[t, i, e * 96 : (e + 1) * 96]

        before = [pltpu.roll(a(h, 0), 1, 1) for h in range(4)]
        mains = []
        for h in range(4):
            after = jnp.where(
                lane96 == 127, pltpu.roll(a(4, 2), 127 - 32 * h, 1), pltpu.roll(a(h, 2), 127, 1)
            )
            mains.append(a(h, 1) + jnp.where(lane96 == 0, 0.0, before[h]) + after)
        left = pltpu.roll(a(4, 0), 1, 1)
        for h in range(4):
            moved = before[h] if h == 0 else pltpu.roll(before[h], 32 * h, 1)
            left = jnp.where(lane96 == 32 * h, moved, left)
        right = jnp.where((lane96 & 31) == 31, 0.0, pltpu.roll(a(4, 2), 127, 1))
        return mains, a(4, 1) + left + right

    stat_ring[0, s, core] = group_sums()
    shared = share_ring(0, (3,))
    arrived(shared)
    stat[0, plane] = stat_ring[0, s, 0] + stat_ring[0, s, 1]
    shared = share_plane(0)
    gain_columns()
    first_rims()
    for t in range(3):
        kept[t] = x1[t + 2, 0:5, own]
    for c in wl1:
        c.wait()
    arrived(rims)
    cached_prepare(x1, t1)
    cached_frames(x1, t1, w1)
    arrived(cached2)
    cached2 = remotes(relay(x2, pl.ds(0, 2)))
    rims2 += remotes(block_halo(x2, pl.ds(0, 2), (1, 3)))
    arrived(shared)
    coefficients(plane_total(0), 0)

    sums[...] = jnp.zeros_like(sums)
    first_copy = taken(36)

    def of_frame(first, moves, t):
        k = first_copy + t * 12 + first
        return [copy_of(k + i, *move) for i, move in enumerate(moves)]

    def middle_spread(t):
        return of_frame(0, spread(x2, t + 2), t)

    def middle_relay(t):
        return of_frame(2, relay(x2, t + 2), t)

    def halo_own(t):
        return of_frame(4, block_halo(x2, t + 2, (0,)), t)

    def halo_near(t):
        return of_frame(6, block_halo(x2, t + 2, (1, 3)), t)

    def halo_far(t):
        return of_frame(10, block_halo(x2, t + 2, (2,)), t)

    def start(copies):
        for c in copies:
            c.start()

    def landed(copies):
        for c in copies:
            c.wait_recv()

    first_far2 = taken(2)
    far2 = [
        copy_of(first_far2 + i, *m) for i, m in enumerate(block_halo(x2, pl.ds(0, 2), (2,)))
    ]

    @pl.loop(0, 3)
    def _(t):
        prepare(x1, t1, t + 2, True)

        @pl.loop(2 - t, 3)
        def _(a):
            conv_step(x1, t1, w1, t + a, a)

        mains, tail = combined(t)
        acc[t] = jnp.zeros((5, 288, 128), F32)
        total1, total2 = sum1[own], sum2[own]
        for h in range(4):
            x2[t + 2, ROW_SLOT[h], own] = mains[h].astype(BF16)
        x2[t + 2, TAIL, own] = tail.astype(BF16)
        start(middle_spread(t))
        start(halo_own(t))
        for v in mains + [tail]:
            total1 = total1 + v
            total2 = total2 + v * v
        sum1[own] = total1
        sum2[own] = total2

        @pl.when(t == 1)
        def _():
            landed(cached2)
            start(far2)

    sent.extend(cached2)
    stat_ring[1, s, core] = group_sums()
    shared = share_ring(1, (5, 1, 4, 6, 0, 2, 3))
    landed(middle_spread(0))
    start(middle_relay(0))
    start(halo_near(0))
    for c in wl2:
        c.wait()
    arrived(rims2 + far2)
    arrived(shared)
    total = stat_ring[1, 0, 0] + stat_ring[1, 0, 1]
    for i in range(1, 4):
        total = total + (stat_ring[1, i, 0] + stat_ring[1, i, 1])
    stat[1, plane] = total
    shared = share_plane(1)
    landed(middle_spread(1))
    start(middle_relay(1))
    start(halo_near(1))
    cached_prepare(x2, t2)
    landed(middle_relay(0))
    start(halo_far(0))
    landed(middle_spread(2))
    start(middle_relay(2))
    start(halo_near(2))
    cached_frames(x2, t2, w2)
    landed(middle_relay(1))
    start(halo_far(1))
    arrived(shared)
    coefficients(plane_total(1), 1)
    gone()

    @pl.loop(0, 3)
    def _(t):
        edges_ = halo_own(t) + halo_near(t) + halo_far(t)
        landed(edges_)
        for c in middle_spread(t) + middle_relay(t) + edges_:
            c.wait_send()
        prepare(x2, t2, t + 2, True)

        @pl.when(t == 0)
        def _():
            landed(middle_relay(2))
            start(halo_far(2))

        @pl.when(t == 0)
        def _():
            conv_taps(x2, t2, w2, 2, 0, 3)

        @pl.when(t == 1)
        def _():
            conv_taps(x2, t2, w2, 3, 1, 2)

        @pl.when(t == 2)
        def _():
            conv_taps(x2, t2, w2, 4, 2, 1)

        mains, tail = combined(t)
        for h in range(4):
            out = (kept[t, ROW_SLOT[h]].astype(F32) + mains[h]).astype(BF16)
            out_ref[t, h] = out
        out = (kept[t, TAIL].astype(F32) + tail).astype(BF16)
        out_ref[t, 4] = out


def channels_last(from_ref, to_ref):
    eye = jnp.where(iota((128, 128), 0) == iota((128, 128), 1), 1.0, 0.0).astype(BF16)
    for h in range(4):
        to_ref[0, h, 0:128] = dot_t(eye, from_ref[0, h]).astype(BF16)
    turned = dot_t(eye, from_ref[0, 4]).astype(BF16)
    for h in range(4):
        to_ref[0, h, 128:160] = turned[32 * h : 32 * h + 32]


def per_device(
    latent,
    row_map,
    latent_cache,
    cache_one,
    cache_two,
    conv_in_w,
    weight_one,
    weight_two,
    gain_one,
    gain_two,
):
    frames, _, channels_in, columns = latent.shape
    entries = float(frames * 128 * GSIZE * columns)
    vmem = pl.BlockSpec(memory_space=pltpu.VMEM)
    hbm = pl.BlockSpec(memory_space=pl.ANY)
    copies = 3 + 2 + 7 + 15 + 1 + 3 + 4 + 4 + 8 + 1 + 15 + 36 + 8 + 7 + 15
    decoded = pl.pallas_call(
        functools.partial(body, entries),
        out_shape=jax.ShapeDtypeStruct((3, 5, 96, 128), BF16),
        in_specs=[vmem, vmem, vmem, vmem, vmem, vmem, hbm, hbm, hbm, hbm],
        out_specs=vmem,
        scratch_shapes=[
            pltpu.VMEM((4, 16, 128), BF16),
            pltpu.VMEM((128, 16, 128), BF16),
            pltpu.VMEM((4, 8, 16, 128), BF16),
            pltpu.VMEM((2, 8, 16, 160), BF16),
            pltpu.VMEM((5, 8, 48, 256), BF16),
            pltpu.VMEM((2, 4, 48, 432), BF16),
            pltpu.VMEM((4, 8, 128), F32),
            pltpu.VMEM((128, 2048), BF16),
            pltpu.VMEM((2, 4, 160, 96), BF16),
            pltpu.VMEM((2, 4, 160, 96), BF16),
            pltpu.VMEM((3, 3, 96, 1152), BF16),
            pltpu.VMEM((3, 3, 96, 1152), BF16),
            pltpu.VMEM((5, 9, 384, 128), BF16),
            pltpu.VMEM((5, 9, 384, 128), BF16),
            pltpu.VMEM((5, 3, 384, 128), BF16),
            pltpu.VMEM((5, 3, 384, 128), BF16),
            pltpu.VMEM((3, 5, 288, 128), F32),
            pltpu.VMEM((3, 5, 96, 128), BF16),
            pltpu.VMEM((768, 128), F32),
            pltpu.VMEM((768, 128), F32),
            pltpu.VMEM((2, 384, 128), F32),
            pltpu.VMEM((3, 128, 768), BF16),
            pltpu.VMEM((384, 128), F32),
            pltpu.VMEM((384, 128), F32),
            pltpu.VMEM((2, 16, 8, 128), F32),
            pltpu.VMEM((2, 4, 2, 8, 128), F32),
            pltpu.SemaphoreType.DMA((copies,)),
            pltpu.SemaphoreType.DMA((copies,)),
            pltpu.SemaphoreType.DMA((8,)),
        ],
        compiler_params=pltpu.CompilerParams(
            collective_id=0, has_side_effects=True, vmem_limit_bytes=56 << 20
        ),
    )(
        row_map.reshape(1, 128),
        latent.reshape(frames, channels_in, columns),
        latent_cache,
        conv_in_w.reshape(27 * channels_in, 96),
        gain_one.reshape(1, 96),
        gain_two.reshape(1, 96),
        jnp.swapaxes(cache_one, 2, 3),
        jnp.swapaxes(cache_two, 2, 3),
        weight_one,
        weight_two,
    )
    decoded = pl.pallas_call(
        channels_last,
        out_shape=jax.ShapeDtypeStruct((3, 4, 160, 96), BF16),
        grid=(3,),
        in_specs=[pl.BlockSpec((1, 5, 96, 128), lambda t: (t, 0, 0, 0))],
        out_specs=pl.BlockSpec((1, 4, 160, 96), lambda t: (t, 0, 0, 0)),
    )(decoded)
    return jnp.swapaxes(decoded, 2, 3)


def solution(mesh):
    torus = Mesh(mesh.devices.reshape(SIZES), AXES)
    all_axes = ("src",) + TILE
    in_specs = (
        P(None, all_axes, None, None),
        P(),
        P(None, TILE, None, None),
        P(None, TILE, "src", None),
        P(None, TILE, "src", None),
        P(None, None, None, None, "src"),
        P(None, None, None, "src", None),
        P(None, None, None, "src", None),
        P("src"),
        P("src"),
    )
    return jax.shard_map(
        per_device,
        mesh=torus,
        in_specs=in_specs,
        out_specs=P(None, TILE, "src", None),
        check_vma=False,
    )
```
